256 devices in a mesh: dp: 32 (over z, y), fsdp: 8 (over x, core).
Axes of the slice: x: 4, y: 4, z: 8, core: 2. Of those that a mesh axis runs over, the one named last changes fastest.
Arguments:
- tokens: bfloat16 [32768, 8192], P('dp', 'fsdp'), may hold values from -6 to 6
- basis: bfloat16 [8192, 512], P('fsdp'), may hold values from -0.0625 to 0.0625
- cotangent: bfloat16 [32768, 29568], P('dp', 'fsdp'), may hold values from -6 to 6
- exp_avg: float32 [512, 29568], P('dp', 'fsdp'), may hold values from -0.0078125 to 0.0078125
- exp_avg_sq: float32 [512, 29568], P('dp', 'fsdp'), may hold values from 1e-09 to 1e-07
Outputs:
- update: bfloat16 [8192, 29568], P('fsdp', 'dp')
- first: float32 [512, 29568], P('dp', 'fsdp')
- second: float32 [512, 29568], P('dp', 'fsdp')
The draws below stay inside these ranges and needn't reach their ends.
All inputs are finite; a program needn't handle non-finite values.
Results may differ from the reference program's by a relative error of at most 0.0074.
Values may be sent and summed in bfloat16 or wider, within the bound.
No kernel may reach another device: no remote copies, remote signals or barrier semaphores. Data moves between devices by JAX's collectives and lax.ppermute only.
A program may use at most 64 MiB of HBM per device.

```python
import math
import jax
import jax.numpy as jnp
from jax import lax

D = 8192
FF = 29568
RANK = 512
TOKENS = 32768


def raised(drawn, key, source, target, shards_of, factor):
    owner, partner = [(jnp.arange(drawn.shape[axis_at]) // (drawn.shape[axis_at] // shards_of)).reshape([-1 if axis == axis_at else 1 for axis in range(drawn.ndim)]) for axis_at in (source, target)]
    chosen = jax.random.permutation(key, shards_of)[partner]
    strong = (owner == chosen) | (owner == (partner + shards_of // 2) % shards_of)
    return jnp.where(strong, factor * drawn, drawn)


def steps_of(rng, dims, cuts, low, largest):
    level, own = 1.0, jax.random.fold_in(rng, 6)
    for dim, shards_of in cuts:
        draws = jnp.exp(jax.random.uniform(jax.random.fold_in(own, dim), (shards_of,), jnp.float32, low / len(cuts), largest / len(cuts)))
        level = level * jnp.repeat(draws, dims[dim] // shards_of).reshape([-1 if axis == dim else 1 for axis in range(len(dims))])
    return level


def noise(rng, extent, scale, limit, shards=(), dtype=jnp.bfloat16):
    level = steps_of(rng, extent, shards, -0.22, 0.18) if shards else 1.0
    values = jax.random.normal(rng, extent, jnp.float32) * scale * level
    return jnp.minimum(jnp.maximum(values, -limit), limit).astype(dtype)


def bell_draw_with(stream_key, dims, scale, limit, split, heavy, dtype=jnp.bfloat16):
    entries = scale * jax.random.normal(stream_key, dims, jnp.float32)
    if split:
        entries = entries * steps_of(stream_key, dims, split, -0.22, 0.18)
    return jnp.clip(raised(entries, jax.random.fold_in(stream_key, 3), *heavy), -limit, limit).astype(dtype)


def setup_inputs(seed: int = 0) -> dict:
    key_of = jax.random.split(jax.random.key(seed), 6)
    tokens = noise(key_of[0], (TOKENS, D), 1.0, 6.0, ((0, 32), (1, 8)))
    basis = noise(key_of[1], (D, RANK), D ** -0.5, 0.0625, ((0, 8),))
    cotangent = bell_draw_with(key_of[2], (TOKENS, FF), 1.0, 6.0, ((0, 32), (1, 8)), (0, 1, 32, 2.75))
    exp_avg = noise(key_of[3], (RANK, FF), 0.0005, 0.0078125, ((0, 32), (1, 8)), jnp.float32)
    exp_avg_sq = jnp.clip(jnp.exp(math.log(1.0000000116860974e-07) - 4.6051702 * jax.random.uniform(key_of[4], (RANK, FF), jnp.float32) ** steps_of(key_of[4], (RANK, FF), ((0, 32), (1, 8)), -0.2, 0.2)), 9.999999717180685e-10, 1.0000000116860974e-07)
    return dict(tokens=tokens, basis=basis, cotangent=cotangent, exp_avg=exp_avg, exp_avg_sq=exp_avg_sq)


bias_first = 1.0 - 0.9 ** 10
bias_second = 1.0 - 0.999 ** 10

def reference(tokens, basis, cotangent, exp_avg, exp_avg_sq):
    proj = jnp.dot(tokens, basis, preferred_element_type=jnp.float32).astype(jnp.bfloat16)
    summed = lax.dot_general(proj, cotangent, (((0,), (0,)), ((), ())), preferred_element_type=jnp.float32)
    grad_low = summed * (1.0 / TOKENS)
    first = 0.9 * exp_avg + 0.1 * grad_low
    second = 0.999 * exp_avg_sq + 0.001 * grad_low * grad_low
    normed = (first / bias_first / (jnp.sqrt(second / bias_second) + 1e-08)).astype(jnp.bfloat16)
    update = jnp.dot(basis, normed, preferred_element_type=jnp.float32).astype(jnp.bfloat16)
    return (update, first, second)
```

```python
import numpy as np
import jax
import jax.numpy as jnp
from jax import lax
from jax.experimental import pallas as pl
from jax.experimental.pallas import tpu as pltpu
from jax.sharding import Mesh, PartitionSpec as P

bias_first = 1.0 - 0.9**10
bias_second = 1.0 - 0.999**10
Z, Y, X, C = 8, 4, 4, 2
f32, bf16 = jnp.float32, jnp.bfloat16


def moved(value, axis, by):
    n = {"z": Z, "y": Y, "x": X, "c": C}[axis]
    return lax.ppermute(value, axis, [(i, (i + by) % n) for i in range(n)])


def owner_rows(device, slot, block, lib):
    z, y, _, c = device
    dy, high = ((2, 0), (2, 1), (1, 1), (3, 0), (1, 0), (3, 1), (0, 1), (0, 0))[slot]
    dz = (4, 5, 3, 6, 2, 7, 1, 0)[slot]
    first = c == 0
    owner_z = lax.rem(z + lib.where(first, 4 * high + block, dz), Z)
    owner_y = lax.rem(y + lib.where(first, dy, block), Y)
    return owner_z, owner_y


def grad_kernel(here, mine_ref, other_ref, cot_ref, *rest):
    outs, held = rest[:-1], rest[-1]
    rows = held.shape[0] // (Z * Y)

    @pl.when(pl.program_id(0) == 0)
    def _():
        device = [here[i] for i in range(4)]
        _, _, x, c = device
        for slot in range(8):
            for block in range(4):
                oz, oy = owner_rows(device, slot, block, jnp)
                at = pl.multiple_of(lax.rem(x + X - lax.rem(oz, X), X) * (Y * rows) + oy * rows, rows)
                mine = lax.div(oz, X) == c
                to = (slot * 4 + block) * rows

                @pl.when(mine)
                def _():
                    held[pl.ds(to, rows), :] = mine_ref[pl.ds(at, rows), :]

                @pl.when(jnp.logical_not(mine))
                def _():
                    held[pl.ds(to, rows), :] = other_ref[pl.ds(at, rows), :]

    g = lax.dot_general(held[...], cot_ref[...], (((1,), (1,)), ((), ())), preferred_element_type=f32)
    unit = held.shape[0] // 8
    for slot, out in enumerate(outs):
        out[...] = g[slot * unit : (slot + 1) * unit].astype(out.dtype)


def gradient(mine, other, cotangent, here):
    half, tokens = mine.shape
    ff = cotangent.shape[1]
    unit, tile = half // 4, min(768, ff)
    whole = lambda i: (0, 0)
    return pl.pallas_call(
        grad_kernel,
        grid=(pl.cdiv(ff, tile),),
        in_specs=[
            pl.BlockSpec(memory_space=pltpu.SMEM),
            pl.BlockSpec((half, tokens), whole),
            pl.BlockSpec((half, tokens), whole),
            pl.BlockSpec((tile, tokens), lambda i: (i, 0)),
        ],
        out_specs=[pl.BlockSpec((unit, tile), lambda i: (0, i))] * 8,
        out_shape=[jax.ShapeDtypeStruct((unit, ff), bf16)] * 2 + [jax.ShapeDtypeStruct((unit, ff), f32)] * 6,
        scratch_shapes=[pltpu.VMEM((2 * half, tokens), bf16)],
        compiler_params=pltpu.CompilerParams(vmem_limit_bytes=40 * 2**20),
        cost_estimate=pl.CostEstimate(
            flops=4 * half * tokens * ff, bytes_accessed=2 * tokens * ff + 14 * half * ff // 2, transcendentals=0
        ),
    )(here, mine, other, cotangent.T)


def near_order(rank):
    c, x = lax.axis_index("c"), lax.axis_index("x")
    part = rank // (X * C)
    n = lax.broadcasted_iota(jnp.int32, (rank, rank), 0)
    r = lax.broadcasted_iota(jnp.int32, (rank, rank), 1)
    chunk = ((c + n // (part * X)) % C) * X + (x + (n // part) % X) % X
    return (r == chunk * part + n % part).astype(bf16)


def project(tokens, basis):
    rank = basis.shape[1]
    half, part = rank // C, rank // (X * C)
    lanes = (((1,), (1,)), ((), ()))
    ordered = lax.dot_general(near_order(rank), basis, lanes, preferred_element_type=f32).astype(bf16)
    away = lax.dot_general(ordered[half:], tokens, lanes, preferred_element_type=f32)
    sent = moved(away, "c", 1)
    both = lax.dot_general(ordered[:half], tokens, lanes, preferred_element_type=f32) + sent
    total = both[:part]
    for got in [moved(both[d * part : (d + 1) * part].astype(bf16), "x", d) for d in (1, 3, 2)]:
        total = total + got.astype(f32)
    mine = total.astype(bf16)
    got = {d: moved(mine, "x", d) for d in (1, 3, 2)}
    mine = jnp.concatenate([mine, got[1], got[2], got[3]], 0)
    return mine, moved(mine, "c", 1)


def crossed(value, by_y, by_z):
    pairs = []
    for z in range(Z):
        for y in range(Y):
            for x in range(X):
                at = lambda z, y, c: (((z % Z) * Y + y % Y) * X + x) * C + c
                if by_y is not None:
                    pairs.append((at(z, y, 0), at(z + by_y[1], y + by_y[0], 0)))
                if by_z is not None:
                    pairs.append((at(z, y, 1), at(z + by_z[1], y + by_z[0], 1)))
    return lax.ppermute(value, ("z", "y", "x", "c"), pairs)


def scatter(p1, m1, p2, m2, p3, m3, p4, own):
    first = lax.axis_index("c") == 0
    up, down = ((1, 0), (0, 1)), ((-1, 0), (0, -1))
    r_p1 = crossed(p1, *up)
    r_m1 = crossed(m1, *down)
    r_p2 = crossed((p2 + jnp.where(first, 0.0, r_p1.astype(f32))).astype(bf16), *up)
    r_m2 = crossed((m2 + jnp.where(first, 0.0, r_m1.astype(f32))).astype(bf16), *down)
    r_p3 = crossed((p3 + jnp.where(first, r_p1, r_p2).astype(f32)).astype(bf16), *up)
    r_m3 = crossed((m3 + jnp.where(first, r_m1, r_m2).astype(f32)).astype(bf16), *down)
    r_p4 = crossed((p4 + r_p3.astype(f32)).astype(bf16), None, (0, 1))
    low = own + jnp.where(first, r_p3.astype(f32) + r_m2.astype(f32), r_p4.astype(f32) + r_m3.astype(f32))
    high = p4 + r_p2.astype(f32) + r_m3.astype(f32)
    rows = own.shape[0] // 4
    total = low[:rows]
    low, high = low.astype(bf16), high.astype(bf16)
    got = [crossed(high[k * rows : (k + 1) * rows], (0, 4 + k), None) for k in (0, 1, 3, 2)]
    got += [crossed(low[k * rows : (k + 1) * rows], (0, k), (k, 0)) for k in (3, 2, 1)]
    for one in got:
        total = total + one.astype(f32)
    return total


def spread(normed):
    c, x = lax.axis_index("c"), lax.axis_index("x")
    _, rows, ff = normed.shape
    cut = normed.reshape(C, rows, Y, ff // Y).transpose(0, 2, 1, 3)
    keep = lax.dynamic_index_in_dim(cut, c, 0, keepdims=False)
    give = lax.dynamic_index_in_dim(cut, 1 - c, 0, keepdims=False)
    swap = moved(give, "c", 1)
    pair = jnp.stack([jnp.where(c == 0, keep, swap), jnp.where(c == 0, swap, keep)])
    wide = jnp.zeros((X,) + pair.shape, bf16)
    wide = lax.dynamic_update_index_in_dim(wide, pair, x, 0)
    for d in (1, 3, 2):
        wide = lax.dynamic_update_index_in_dim(wide, moved(pair, "x", d), (x - d) % X, 0)
    wide = wide.reshape(X * C * Y, rows, ff // Y)
    mine = lax.all_to_all(wide, ("z", "y"), 0, 0, tiled=True)
    other = moved(mine, "c", 1)
    return jnp.stack([jnp.where(c == 0, mine, other), jnp.where(c == 0, other, mine)])


def shards(tokens, basis, cotangent, exp_avg, exp_avg_sq):
    rank, ff = basis.shape[1], cotangent.shape[1]
    rows = rank // (2 * Z * Y)
    here = jnp.stack([lax.axis_index(axis) for axis in ("z", "y", "x", "c")]).astype(jnp.int32)
    mine, other = project(tokens, basis)
    total = scatter(*gradient(mine, other, cotangent, here))
    total_tokens = cotangent.shape[0] * Z * Y
    grad_low = total * (1.0 / total_tokens)
    first = 0.9 * exp_avg + 0.1 * grad_low
    second = 0.999 * exp_avg_sq + 0.001 * grad_low * grad_low
    normed = (first / bias_first / (jnp.sqrt(second / bias_second) + 1e-08)).astype(bf16)
    all_rows = spread(normed.reshape(2, rows, ff)).reshape(rank, ff // Y)
    by_half = basis.reshape(-1, Z * Y, 2, rows).transpose(0, 2, 1, 3).reshape(-1, rank)
    update = jnp.dot(by_half, all_rows, preferred_element_type=f32).astype(bf16)
    return (update, first, second)


def solution(mesh):
    fine = Mesh(np.asarray(mesh.devices).reshape(Z, Y, X, C), ("z", "y", "x", "c"))
    dp, fsdp = ("z", "y"), ("x", "c")
    in_specs = (P(dp, fsdp), P(fsdp, None), P(dp, fsdp), P(dp, fsdp), P(dp, fsdp))
    out_specs = (P(fsdp, dp), P(dp, fsdp), P(dp, fsdp))
    return jax.shard_map(shards, mesh=fine, in_specs=in_specs, out_specs=out_specs, check_vma=False)
```

```python
import numpy as np
import jax
import jax.numpy as jnp
from jax import lax
from jax.experimental import pallas as pl
from jax.experimental.pallas import tpu as pltpu
from jax.sharding import Mesh, PartitionSpec as P

bias_first = 1.0 - 0.9**10
bias_second = 1.0 - 0.999**10
Z, Y, X, C = 8, 4, 4, 2
f32, bf16 = jnp.float32, jnp.bfloat16


def moved(value, axis, by):
    n = {"z": Z, "y": Y, "x": X, "c": C}[axis]
    return lax.ppermute(value, axis, [(i, (i + by) % n) for i in range(n)])


def owner_rows(device, slot, block, lib):
    z, y, _, c = device
    dy, high = ((2, 0), (2, 1), (1, 1), (3, 0), (1, 0), (3, 1), (0, 1), (0, 0))[slot]
    dz = (4, 5, 3, 6, 2, 7, 1, 0)[slot]
    first = c == 0
    pair = z + 1 - 2 * lax.rem(z, 2)
    owner_z = lax.rem(lib.where(first, (pair if high else z) + 2 * block, z + dz), Z)
    owner_y = lax.rem(y + lib.where(first, dy, block), Y)
    return owner_z, owner_y


def grad_kernel(here, mine_ref, other_ref, cot_ref, *rest):
    outs, held = rest[:-1], rest[-1]
    rows = held.shape[0] // (Z * Y)

    @pl.when(pl.program_id(0) == 0)
    def _():
        device = [here[i] for i in range(4)]
        _, _, x, c = device
        for slot in range(8):
            for block in range(4):
                oz, oy = owner_rows(device, slot, block, jnp)
                at = pl.multiple_of(lax.rem(x + X - lax.rem(oz, X), X) * (Y * rows) + oy * rows, rows)
                mine = lax.div(oz, X) == c
                to = (slot * 4 + block) * rows

                block_here, block_there = mine_ref[pl.ds(at, rows), :], other_ref[pl.ds(at, rows), :]
                held[pl.ds(to, rows), :] = jnp.where(mine, block_here, block_there)

    g = lax.dot_general(held[...], cot_ref[...], (((1,), (1,)), ((), ())), preferred_element_type=f32)
    unit = held.shape[0] // 8
    for slot, out in enumerate(outs):
        out[...] = g[slot * unit : (slot + 1) * unit].astype(out.dtype)


def gradient(mine, other, cotangent, here):
    half, tokens = mine.shape
    ff = cotangent.shape[1]
    unit, tile = half // 4, min(1280, ff)
    whole = lambda i: (0, 0)
    return pl.pallas_call(
        grad_kernel,
        grid=(pl.cdiv(ff, tile),),
        in_specs=[
            pl.BlockSpec(memory_space=pltpu.SMEM),
            pl.BlockSpec((half, tokens), whole),
            pl.BlockSpec((half, tokens), whole),
            pl.BlockSpec((tile, tokens), lambda i: (i, 0)),
        ],
        out_specs=[pl.BlockSpec((unit, tile), lambda i: (0, i))] * 8,
        out_shape=[jax.ShapeDtypeStruct((unit, ff), bf16)] * 2 + [jax.ShapeDtypeStruct((unit, ff), f32)] * 6,
        scratch_shapes=[pltpu.VMEM((2 * half, tokens), bf16)],
        compiler_params=pltpu.CompilerParams(vmem_limit_bytes=20 * 2**20),
        cost_estimate=pl.CostEstimate(
            flops=4 * half * tokens * ff, bytes_accessed=2 * tokens * ff + 14 * half * ff // 2, transcendentals=0
        ),
    )(here, mine, other, cotangent.T)


def near_order(rank):
    c, x = lax.axis_index("c"), lax.axis_index("x")
    part = rank // (X * C)
    n = lax.broadcasted_iota(jnp.int32, (rank, rank), 0)
    r = lax.broadcasted_iota(jnp.int32, (rank, rank), 1)
    chunk = ((c + n // (part * X)) % C) * X + (x + (n // part) % X) % X
    return (r == chunk * part + n % part).astype(bf16)


def project(tokens, basis):
    rank = basis.shape[1]
    half, part = rank // C, rank // (X * C)
    lanes = (((1,), (1,)), ((), ()))
    ordered = lax.dot_general(near_order(rank), basis, lanes, preferred_element_type=f32).astype(bf16)
    away = lax.dot_general(ordered[half:], tokens, lanes, preferred_element_type=f32)
    sent = moved(away, "c", 1)
    both = lax.dot_general(ordered[:half], tokens, lanes, preferred_element_type=f32) + sent
    total = both[:part]
    for got in [moved(both[d * part : (d + 1) * part].astype(bf16), "x", d) for d in (1, 3, 2)]:
        total = total + got.astype(f32)
    mine = total.astype(bf16)
    got = {d: moved(mine, "x", d) for d in (1, 3, 2)}
    mine = jnp.concatenate([mine, got[1], got[2], got[3]], 0)
    return mine, moved(mine, "c", 1)


def crossed(value, by_y, by_z):
    pairs = []
    for z in range(Z):
        for y in range(Y):
            for x in range(X):
                at = lambda z, y, c: (((z % Z) * Y + y % Y) * X + x) * C + c
                if by_y is not None:
                    pairs.append((at(z, y, 0), at(z + by_y[1], y + by_y[0], 0)))
                if by_z is not None:
                    pairs.append((at(z, y, 1), at(z + by_z[1], y + by_z[0], 1)))
    return lax.ppermute(value, ("z", "y", "x", "c"), pairs)


def scatter(p1, m1, p2, m2, p3, m3, p4, own):
    first = lax.axis_index("c") == 0
    up, down = ((1, 0), (0, 1)), ((-1, 0), (0, -1))
    r_p1 = crossed(p1, *up)
    r_m1 = crossed(m1, *down)
    r_p2 = crossed((p2 + jnp.where(first, 0.0, r_p1.astype(f32))).astype(bf16), *up)
    r_m2 = crossed((m2 + jnp.where(first, 0.0, r_m1.astype(f32))).astype(bf16), *down)
    r_p3 = crossed((p3 + jnp.where(first, r_p1, r_p2).astype(f32)).astype(bf16), *up)
    r_m3 = crossed((m3 + jnp.where(first, r_m1, r_m2).astype(f32)).astype(bf16), *down)
    r_p4 = crossed((p4 + r_p3.astype(f32)).astype(bf16), None, (0, 1))
    low = own + jnp.where(first, r_p3.astype(f32) + r_m2.astype(f32), r_p4.astype(f32) + r_m3.astype(f32))
    high = (p4 + r_p2.astype(f32) + r_m3.astype(f32)).astype(bf16)
    low = low + paired(high).astype(f32)
    rows = own.shape[0] // 4
    total, low = low[:rows], low.astype(bf16)
    for k in (2, 1, 3):
        total = total + crossed(low[k * rows : (k + 1) * rows], (0, 2 * k), (k, 0)).astype(f32)
    return total


def paired(value):
    at = lambda z, rest: (z * Y * X + rest) * C
    return lax.ppermute(value, ("z", "y", "x", "c"), [(at(z, r), at(z ^ 1, r)) for z in range(Z) for r in range(Y * X)])


def picked(choices, index):
    out = choices[0]
    for k in range(1, len(choices)):
        out = jnp.where(index == k, choices[k], out)
    return out


def spread(normed):
    z, y, x, c = (lax.axis_index(axis) for axis in ("z", "y", "x", "c"))
    rows, ff = normed.shape
    cut = normed.reshape(rows, Y, ff // Y).transpose(1, 0, 2)
    piece = lambda k: lax.dynamic_index_in_dim(cut, (y + k) % Y, 0, keepdims=False)
    got = {d: moved(piece(d), "y", d) for d in (1, 3, 2)}
    tall = jnp.stack([piece(0), got[1], got[2], got[3]])
    got = {d: moved(tall, "x", d) for d in (1, 3, 2)}
    wide = [tall, got[1], got[2], got[3]]
    odd = (z + c) % 2
    half = []
    for k in (0, 1, 2, 3):
        to = (z + 2 * k + odd) % Z
        sent = picked(wide, (x - to // 2) % X)
        pairs = []
        for pz in range(Z):
            for pc in range(C):
                po = (pz + pc) % 2
                for r in range(Y * X):
                    if k or po:
                        pairs.append(((pz * Y * X + r) * C + pc, (((pz + 2 * k + po) % Z) * Y * X + r) * C + (pc ^ po)))
        moved_in = lax.ppermute(sent, ("z", "y", "x", "c"), pairs)
        half.append(moved_in if k else jnp.where(odd == 0, sent, moved_in))
    half = jnp.stack(half)
    return half, moved(half, "c", 1)


def spread_order(rank):
    z, y, c = (lax.axis_index(axis) for axis in ("z", "y", "c"))
    rows = rank // (Z * Y)
    n = lax.broadcasted_iota(jnp.int32, (rank, rank), 1)
    r = lax.broadcasted_iota(jnp.int32, (rank, rank), 0)
    h, k, j = n // (rank // 2), (n // (rows * Y)) % (Z // 2), (n // rows) % Y
    owner_z = (z + 2 * Z - 2 * k - (z + c + h) % 2) % Z
    want = (owner_z * Y + (y + Y - j) % Y) * rows + n % rows
    return (r == want).astype(bf16)


def shards(tokens, basis, cotangent, exp_avg, exp_avg_sq):
    rank, ff = basis.shape[1], cotangent.shape[1]
    here = jnp.stack([lax.axis_index(axis) for axis in ("z", "y", "x", "c")]).astype(jnp.int32)
    mine, other = project(tokens, basis)
    total = scatter(*gradient(mine, other, cotangent, here))
    total_tokens = cotangent.shape[0] * Z * Y
    grad_low = total * (1.0 / total_tokens)
    first = 0.9 * exp_avg + 0.1 * grad_low
    second = 0.999 * exp_avg_sq + 0.001 * grad_low * grad_low
    normed = (first / bias_first / (jnp.sqrt(second / bias_second) + 1e-08)).astype(bf16)
    all_rows = jnp.stack(spread(normed)).reshape(rank, ff // Y)
    ordered = jnp.dot(basis, spread_order(rank), preferred_element_type=f32).astype(bf16)
    update = jnp.dot(ordered, all_rows, preferred_element_type=f32).astype(bf16)
    return (update, first, second)


def solution(mesh):
    fine = Mesh(np.asarray(mesh.devices).reshape(Z, Y, X, C), ("z", "y", "x", "c"))
    dp, fsdp = ("z", "y"), ("x", "c")
    in_specs = (P(dp, fsdp), P(fsdp, None), P(dp, fsdp), P(dp, fsdp), P(dp, fsdp))
    out_specs = (P(fsdp, dp), P(dp, fsdp), P(dp, fsdp))
    return jax.shard_map(shards, mesh=fine, in_specs=in_specs, out_specs=out_specs, check_vma=False)
```

```python
import numpy as np
import jax
import jax.numpy as jnp
from jax import lax
from jax.experimental import pallas as pl
from jax.experimental.pallas import tpu as pltpu
from jax.sharding import Mesh, PartitionSpec as P

bias_first = 1.0 - 0.9**10
bias_second = 1.0 - 0.999**10
Z, Y, X, C = 8, 4, 4, 2
f32, bf16 = jnp.float32, jnp.bfloat16


def moved(value, axis, by):
    n = {"z": Z, "y": Y, "x": X, "c": C}[axis]
    return lax.ppermute(value, axis, [(i, (i + by) % n) for i in range(n)])


def grad_kernel(here, mine_ref, other_ref, cot_ref, *rest):
    outs, held = rest[:-1], rest[-1]
    rows = held.shape[0] // (Z * Y)

    @pl.when(pl.program_id(0) == 0)
    def _():
        z, y, x, c = (here[i] for i in range(4))
        for dy in range(Y):
            for dz in range(Z):
                oz, oy = lax.rem(z + dz, Z), lax.rem(y + dy, Y)
                at = pl.multiple_of(lax.rem(x + X - lax.rem(oz, X), X) * (Y * rows) + oy * rows, rows)
                block_here, block_there = mine_ref[pl.ds(at, rows), :], other_ref[pl.ds(at, rows), :]
                held[pl.ds((dy * Z + dz) * rows, rows), :] = jnp.where(lax.div(oz, X) == c, block_here, block_there)

    g = lax.dot_general(held[...], cot_ref[...], (((1,), (1,)), ((), ())), preferred_element_type=f32)
    part = rows // 2
    for out, places in zip(outs, UNITS):
        pieces = [g[(dy * Z + dz) * rows + s * part :][:part] for dy, dz, s in places]
        if out.dtype == f32:
            for i, piece in enumerate(pieces):
                out[i * part : (i + 1) * part, :] = piece
        else:
            out[...] = jnp.concatenate(pieces, 0).astype(out.dtype)


EVEN, ODD = (0, 2, 4, 6), (1, 3, 5, 7)
UNITS = [[(2, dz, 0) for dz in EVEN], [(2, dz, 0) for dz in ODD]]
UNITS += [[(dy, dz, 0) for dz in EVEN + ODD] for dy in (1, 3, 0)]
UNITS += [[(dy, dz, 1) for dy in range(Y)] for dz in (4, 5, 3, 6, 2, 7, 1, 0)]
ROUNDED = (0, 1, 5, 6)


def gradient(mine, other, cotangent, here):
    half, tokens = mine.shape
    ff = cotangent.shape[1]
    part, tile = half // (Z * Y), min(1280, ff)
    whole = lambda i: (0, 0)
    shapes = [(len(places) * part, bf16 if k in ROUNDED else f32) for k, places in enumerate(UNITS)]
    cot = pltpu.with_memory_space_constraint(cotangent.T, pltpu.HBM)
    mine = pltpu.with_memory_space_constraint(mine, pltpu.HBM)
    other = pltpu.with_memory_space_constraint(other, pltpu.HBM)
    return pl.pallas_call(
        grad_kernel,
        grid=(pl.cdiv(ff, tile),),
        in_specs=[
            pl.BlockSpec(memory_space=pltpu.SMEM),
            pl.BlockSpec((half, tokens), whole),
            pl.BlockSpec((half, tokens), whole),
            pl.BlockSpec((tile, tokens), lambda i: (i, 0)),
        ],
        out_specs=[pl.BlockSpec((n, tile), lambda i: (0, i)) for n, _ in shapes],
        out_shape=[pltpu.HBM((n, ff), t) for n, t in shapes],
        scratch_shapes=[pltpu.VMEM((2 * half, tokens), bf16)],
        compiler_params=pltpu.CompilerParams(vmem_limit_bytes=24 * 2**20),
        cost_estimate=pl.CostEstimate(
            flops=4 * half * tokens * ff, bytes_accessed=2 * tokens * ff + 14 * half * ff // 2, transcendentals=0
        ),
    )(here, mine, other, cot)


def near_order(rank):
    c, x = lax.axis_index("c"), lax.axis_index("x")
    part = rank // (X * C)
    n = lax.broadcasted_iota(jnp.int32, (rank, rank), 0)
    r = lax.broadcasted_iota(jnp.int32, (rank, rank), 1)
    chunk = ((c + n // (part * X)) % C) * X + (x + (n // part) % X) % X
    return (r == chunk * part + n % part).astype(bf16)


def project(tokens, basis):
    rank = basis.shape[1]
    half, part = rank // C, rank // (X * C)
    lanes = (((1,), (1,)), ((), ()))
    ordered = lax.dot_general(near_order(rank), basis, lanes, preferred_element_type=f32).astype(bf16)
    away = lax.dot_general(ordered[half:], tokens, lanes, preferred_element_type=f32)
    sent = moved(away, "c", 1)
    both = lax.dot_general(ordered[:half], tokens, lanes, preferred_element_type=f32) + sent
    total = both[:part]
    for got in [moved(both[d * part : (d + 1) * part].astype(bf16), "x", d) for d in (1, 3, 2)]:
        total = total + got.astype(f32)
    mine = total.astype(bf16)
    got = {d: moved(mine, "x", d) for d in (1, 3, 2)}
    mine = jnp.concatenate([mine, got[1], got[2], got[3]], 0)
    return mine, moved(mine, "c", 1)


def scatter_y_first(two_low, two_high, one, three, zero):
    h = two_low.shape[0]
    up, down = moved(two_low, "y", 1).astype(f32), moved(two_high, "y", -1).astype(f32)
    up = moved(jnp.concatenate([one[:h] + up, one[h:]], 0).astype(bf16), "y", 1)
    down = moved(jnp.concatenate([three[:h], three[h:] + down], 0).astype(bf16), "y", -1)
    low = zero[:h] + up[:h].astype(f32) + down[:h].astype(f32)
    high = zero[h:] + up[h:].astype(f32) + down[h:].astype(f32)
    rows = h // 4
    got = lax.ppermute(high.astype(bf16), "z", [(z, z ^ 1) for z in range(Z)]).astype(f32)
    turned = jnp.concatenate([got[-rows:], got[:-rows]], 0)
    low = low + jnp.where(lax.axis_index("z") % 2 == 0, turned, got)
    total, low = low[:rows], low.astype(bf16)
    for k in (2, 1, 3):
        total = total + moved(low[k * rows : (k + 1) * rows], "z", 2 * k).astype(f32)
    return total


def scatter_z_first(four, five, three, six, two, seven, one, zero):
    up, down = moved(four, "z", 1), moved(five, "z", -1)
    for k, m in ((three, six), (two, seven)):
        up = moved((k + up.astype(f32)).astype(bf16), "z", 1)
        down = moved((m + down.astype(f32)).astype(bf16), "z", -1)
    up = moved((one + up.astype(f32)).astype(bf16), "z", 1)
    total = zero + up.astype(f32) + down.astype(f32)
    rows = zero.shape[0] // Y
    total, rounded = total[:rows], total.astype(bf16)
    for k in (2, 1, 3):
        total = total + moved(rounded[k * rows : (k + 1) * rows], "y", k).astype(f32)
    return total


def picked(choices, index):
    out = choices[0]
    for k in range(1, len(choices)):
        out = jnp.where(index == k, choices[k], out)
    return out


def spread(normed):
    z, y, x, c = (lax.axis_index(axis) for axis in ("z", "y", "x", "c"))
    rows, ff = normed.shape
    cut = normed.reshape(rows, Y, ff // Y).transpose(1, 0, 2)
    piece = lambda k: lax.dynamic_index_in_dim(cut, (y + k) % Y, 0, keepdims=False)
    got = {d: moved(piece(d), "y", d) for d in (1, 3, 2)}
    tall = jnp.stack([piece(0), got[1], got[2], got[3]])
    got = {d: moved(tall, "x", d) for d in (1, 3, 2)}
    wide = [tall, got[1], got[2], got[3]]
    odd = (z + c) % 2
    half = []
    for k in (0, 1, 2, 3):
        to = (z + 2 * k + odd) % Z
        sent = picked(wide, (x - to // 2) % X)
        pairs = []
        for pz in range(Z):
            for pc in range(C):
                po = (pz + pc) % 2
                for r in range(Y * X):
                    if k or po:
                        pairs.append(((pz * Y * X + r) * C + pc, (((pz + 2 * k + po) % Z) * Y * X + r) * C + (pc ^ po)))
        moved_in = lax.ppermute(sent, ("z", "y", "x", "c"), pairs)
        half.append(moved_in if k else jnp.where(odd == 0, sent, moved_in))
    half = jnp.stack(half)
    return half, moved(half, "c", 1)


def spread_order(rank):
    z, y, c = (lax.axis_index(axis) for axis in ("z", "y", "c"))
    rows = rank // (Z * Y)
    n = lax.broadcasted_iota(jnp.int32, (rank, rank), 1)
    r = lax.broadcasted_iota(jnp.int32, (rank, rank), 0)
    h, k, j = n // (rank // 2), (n // (rows * Y)) % (Z // 2), (n // rows) % Y
    owner_z = (z + 2 * Z - 2 * k - (z + c + h) % 2) % Z
    want = (owner_z * Y + (y + Y - j) % Y) * rows + n % rows
    return (r == want).astype(bf16)


def shards(tokens, basis, cotangent, exp_avg, exp_avg_sq):
    rank, ff = basis.shape[1], cotangent.shape[1]
    here = jnp.stack([lax.axis_index(axis) for axis in ("z", "y", "x", "c")]).astype(jnp.int32)
    mine, other = project(tokens, basis)
    units = gradient(mine, other, cotangent, here)
    total = jnp.concatenate([scatter_y_first(*units[:5]), scatter_z_first(*units[5:])], 0)
    total_tokens = cotangent.shape[0] * Z * Y
    grad_low = total * (1.0 / total_tokens)
    first = 0.9 * exp_avg + 0.1 * grad_low
    second = 0.999 * exp_avg_sq + 0.001 * grad_low * grad_low
    normed = (first / bias_first / (jnp.sqrt(second / bias_second) + 1e-08)).astype(bf16)
    all_rows = jnp.stack(spread(normed)).reshape(rank, ff // Y)
    ordered = jnp.dot(basis, spread_order(rank), preferred_element_type=f32).astype(bf16)
    update = jnp.dot(ordered, all_rows, preferred_element_type=f32).astype(bf16)
    return (update, first, second)


def solution(mesh):
    fine = Mesh(np.asarray(mesh.devices).reshape(Z, Y, X, C), ("z", "y", "x", "c"))
    dp, fsdp = ("z", "y"), ("x", "c")
    in_specs = (P(dp, fsdp), P(fsdp, None), P(dp, fsdp), P(dp, fsdp), P(dp, fsdp))
    out_specs = (P(fsdp, dp), P(dp, fsdp), P(dp, fsdp))
    return jax.shard_map(shards, mesh=fine, in_specs=in_specs, out_specs=out_specs, check_vma=False)
```

```python
import functools

import numpy as np
import jax
import jax.numpy as jnp
from jax import lax
from jax.experimental import pallas as pl
from jax.experimental.pallas import tpu as pltpu
from jax.sharding import Mesh, PartitionSpec as P

bias_first = 1.0 - 0.9**10
bias_second = 1.0 - 0.999**10
Z, Y, X, C = 8, 4, 4, 2
f32, bf16 = jnp.float32, jnp.bfloat16


def moved(value, axis, by):
    n = {"z": Z, "y": Y, "x": X, "c": C}[axis]
    return lax.ppermute(value, axis, [(i, (i + by) % n) for i in range(n)])


EVEN, ODD = (0, 2, 4, 6), (1, 3, 5, 7)
Y_FIRST = [[(2, dz) for dz in EVEN], [(2, dz) for dz in ODD]] + [[(dy, dz) for dz in EVEN + ODD] for dy in (1, 3, 0)]
Z_FIRST = [[(dy, dz) for dy in range(Y)] for dz in (4, 5, 3, 6, 2, 7, 1, 0)]


def grad_kernel(units, here, mine_ref, other_ref, cot_ref, *rest):
    outs, held = rest[:-1], rest[-1]
    block = held.shape[0] // Z
    rows = block // Y

    @pl.when(pl.program_id(0) == 0)
    def _():
        x, c = here[0], here[1]
        for dz in range(Z):
            at = pl.multiple_of(lax.rem(x + X - dz % X, X) * block, block)
            block_here, block_there = mine_ref[pl.ds(at, block), :], other_ref[pl.ds(at, block), :]
            held[dz * block : (dz + 1) * block, :] = jnp.where(c == dz // X, block_here, block_there)

    g = lax.dot_general(held[...], cot_ref[...], (((1,), (1,)), ((), ())), preferred_element_type=f32)
    for out, places in zip(outs, units):
        pieces = [g[dz * block + dy * rows :][:rows] for dy, dz in places]
        if out.dtype == f32:
            for i, piece in enumerate(pieces):
                out[i * rows : (i + 1) * rows, :] = piece
        else:
            out[...] = jnp.concatenate(pieces, 0).astype(out.dtype)


def gradient(units, mine, other, cotangent, here):
    half, tokens = mine.shape
    ff = cotangent.shape[1]
    rows, tile = 2 * half // (Z * Y), min(1280, ff)
    whole = lambda i: (0, 0)
    shapes = [(len(places) * rows, f32 if k > 1 else bf16) for k, places in enumerate(units)]
    in_hbm = lambda v: pltpu.with_memory_space_constraint(v, pltpu.HBM)
    return pl.pallas_call(
        functools.partial(grad_kernel, units),
        grid=(pl.cdiv(ff, tile),),
        in_specs=[
            pl.BlockSpec(memory_space=pltpu.SMEM),
            pl.BlockSpec((half, tokens), whole),
            pl.BlockSpec((half, tokens), whole),
            pl.BlockSpec((tile, tokens), lambda i: (i, 0)),
        ],
        out_specs=[pl.BlockSpec((n, tile), lambda i: (0, i)) for n, _ in shapes],
        out_shape=[pltpu.HBM((n, ff), t) for n, t in shapes],
        scratch_shapes=[pltpu.VMEM((2 * half, tokens), bf16)],
        compiler_params=pltpu.CompilerParams(vmem_limit_bytes=20 * 2**20),
        cost_estimate=pl.CostEstimate(
            flops=4 * half * tokens * ff, bytes_accessed=2 * tokens * ff + 14 * half * ff // 2, transcendentals=0
        ),
    )(here, in_hbm(mine), in_hbm(other), in_hbm(cotangent.T))


def near_order(rank, s):
    z, y, x, c = (lax.axis_index(axis) for axis in ("z", "y", "x", "c"))
    rows = rank // (2 * Z * Y)
    n = lax.broadcasted_iota(jnp.int32, (rank // 2, rank), 0)
    r = lax.broadcasted_iota(jnp.int32, (rank // 2, rank), 1)
    dz = (c + n // (rows * Y * X)) % C * X + (x + n // (rows * Y)) % X
    owner = (z + dz) % Z * Y + (y + n // rows) % Y
    return (r == owner * (2 * rows) + s * rows + n % rows).astype(bf16)


def project(tokens, basis, s):
    rank = basis.shape[1]
    half, part = rank // 2 // C, rank // 2 // (X * C)
    lanes = (((1,), (1,)), ((), ()))
    ordered = lax.dot_general(near_order(rank, s), basis, lanes, preferred_element_type=f32).astype(bf16)
    away = lax.dot_general(ordered[half:], tokens, lanes, preferred_element_type=f32)
    sent = moved(away, "c", 1)
    both = lax.dot_general(ordered[:half], tokens, lanes, preferred_element_type=f32) + sent
    total = both[:part]
    for got in [moved(both[d * part : (d + 1) * part].astype(bf16), "x", d) for d in (1, 3, 2)]:
        total = total + got.astype(f32)
    mine = total.astype(bf16)
    got = {d: moved(mine, "x", d) for d in (1, 3, 2)}
    mine = jnp.concatenate([mine, got[1], got[2], got[3]], 0)
    return mine, moved(mine, "c", 1)


def scatter_y_first(two_low, two_high, one, three, zero):
    h = two_low.shape[0]
    up, down = moved(two_low, "y", 1).astype(f32), moved(two_high, "y", -1).astype(f32)
    up = moved(jnp.concatenate([one[:h] + up, one[h:]], 0).astype(bf16), "y", 1)
    down = moved(jnp.concatenate([three[:h], three[h:] + down], 0).astype(bf16), "y", -1)
    low = zero[:h] + up[:h].astype(f32) + down[:h].astype(f32)
    high = zero[h:] + up[h:].astype(f32) + down[h:].astype(f32)
    rows = h // 4
    got = lax.ppermute(high.astype(bf16), "z", [(z, z ^ 1) for z in range(Z)]).astype(f32)
    turned = jnp.concatenate([got[-rows:], got[:-rows]], 0)
    low = low + jnp.where(lax.axis_index("z") % 2 == 0, turned, got)
    total, low = low[:rows], low.astype(bf16)
    for k in (2, 1, 3):
        total = total + moved(low[k * rows : (k + 1) * rows], "z", 2 * k).astype(f32)
    return total


def scatter_z_first(four, five, three, six, two, seven, one, zero):
    up, down = moved(four, "z", 1), moved(five, "z", -1)
    for k, m in ((three, six), (two, seven)):
        up = moved((k + up.astype(f32)).astype(bf16), "z", 1)
        down = moved((m + down.astype(f32)).astype(bf16), "z", -1)
    up = moved((one + up.astype(f32)).astype(bf16), "z", 1)
    total = zero + up.astype(f32) + down.astype(f32)
    rows = zero.shape[0] // Y
    total, rounded = total[:rows], total.astype(bf16)
    for k in (2, 1, 3):
        total = total + moved(rounded[k * rows : (k + 1) * rows], "y", k).astype(f32)
    return total


def picked(choices, index):
    out = choices[0]
    for k in range(1, len(choices)):
        out = jnp.where(index == k, choices[k], out)
    return out


def spread(normed):
    z, y, x, c = (lax.axis_index(axis) for axis in ("z", "y", "x", "c"))
    rows, ff = normed.shape
    cut = normed.reshape(rows, Y, ff // Y).transpose(1, 0, 2)
    piece = lambda k: lax.dynamic_index_in_dim(cut, (y + k) % Y, 0, keepdims=False)
    got = {d: moved(piece(d), "y", d) for d in (1, 3, 2)}
    tall = jnp.stack([piece(0), got[1], got[2], got[3]])
    got = {d: moved(tall, "x", d) for d in (1, 3, 2)}
    wide = [tall, got[1], got[2], got[3]]
    odd = (z + c) % 2
    half = []
    for k in (0, 1, 2, 3):
        to = (z + 2 * k + odd) % Z
        sent = picked(wide, (x - to // 2) % X)
        pairs = []
        for pz in range(Z):
            for pc in range(C):
                po = (pz + pc) % 2
                for r in range(Y * X):
                    if k or po:
                        pairs.append(((pz * Y * X + r) * C + pc, (((pz + 2 * k + po) % Z) * Y * X + r) * C + (pc ^ po)))
        moved_in = lax.ppermute(sent, ("z", "y", "x", "c"), pairs)
        half.append(moved_in if k else jnp.where(odd == 0, sent, moved_in))
    half = jnp.stack(half)
    return half, moved(half, "c", 1)


def spread_order(rank, s):
    z, y, c = (lax.axis_index(axis) for axis in ("z", "y", "c"))
    rows = rank // (2 * Z * Y)
    n = lax.broadcasted_iota(jnp.int32, (rank, rank // 2), 1)
    r = lax.broadcasted_iota(jnp.int32, (rank, rank // 2), 0)
    h, k, j = n // (rank // 4), (n // (rows * Y)) % (Z // 2), (n // rows) % Y
    owner_z = (z + 2 * Z - 2 * k - (z + c + h) % 2) % Z
    want = (owner_z * Y + (y + Y - j) % Y) * (2 * rows) + s * rows + n % rows
    return (r == want).astype(bf16)


def shards(tokens, basis, cotangent, exp_avg, exp_avg_sq):
    rank, ff = basis.shape[1], cotangent.shape[1]
    rows = exp_avg.shape[0] // 2
    total_tokens = cotangent.shape[0] * Z * Y
    here = jnp.stack([lax.axis_index("x"), lax.axis_index("c")]).astype(jnp.int32)
    firsts, seconds, products = [None] * 2, [None] * 2, []
    for s, units, scatter in ((1, Z_FIRST, scatter_z_first), (0, Y_FIRST, scatter_y_first)):
        mine, other = project(tokens, basis, s)
        grad_low = scatter(*gradient(units, mine, other, cotangent, here)) * (1.0 / total_tokens)
        first = 0.9 * exp_avg[s * rows : (s + 1) * rows] + 0.1 * grad_low
        second = 0.999 * exp_avg_sq[s * rows : (s + 1) * rows] + 0.001 * grad_low * grad_low
        normed = (first / bias_first / (jnp.sqrt(second / bias_second) + 1e-08)).astype(bf16)
        firsts[s], seconds[s] = first, second
        ordered = jnp.dot(basis, spread_order(rank, s), preferred_element_type=f32).astype(bf16)
        for h, got in enumerate(spread(normed)):
            part = ordered[:, h * (rank // 4) : (h + 1) * (rank // 4)]
            products.append(jnp.dot(part, got.reshape(rank // 4, ff // Y), preferred_element_type=f32))
    update = (((products[0] + products[1]) + products[2]) + products[3]).astype(bf16)
    return (update, jnp.concatenate(firsts, 0), jnp.concatenate(seconds, 0))


def solution(mesh):
    fine = Mesh(np.asarray(mesh.devices).reshape(Z, Y, X, C), ("z", "y", "x", "c"))
    dp, fsdp = ("z", "y"), ("x", "c")
    in_specs = (P(dp, fsdp), P(fsdp, None), P(dp, fsdp), P(dp, fsdp), P(dp, fsdp))
    out_specs = (P(fsdp, dp), P(dp, fsdp), P(dp, fsdp))
    return jax.shard_map(shards, mesh=fine, in_specs=in_specs, out_specs=out_specs, check_vma=False)
```

```python
import numpy as np
import jax
import jax.numpy as jnp
from jax import lax
from jax.experimental import pallas as pl
from jax.experimental.pallas import tpu as pltpu
from jax.sharding import Mesh, PartitionSpec as P

bias_first = 1.0 - 0.9**10
bias_second = 1.0 - 0.999**10
Z, Y, X, C = 8, 4, 4, 2
f32, bf16 = jnp.float32, jnp.bfloat16


def moved(value, axis, by):
    n = {"z": Z, "y": Y, "x": X, "c": C}[axis]
    return lax.ppermute(value, axis, [(i, (i + by) % n) for i in range(n)])


def grad_kernel(here, mine_ref, other_ref, cot_ref, *rest):
    outs, held = rest[:-1], rest[-1]
    rows = held.shape[0] // (Z * Y)

    @pl.when(pl.program_id(0) == 0)
    def _():
        z, y, x, c = (here[i] for i in range(4))
        for dy in range(Y):
            for dz in range(Z):
                oz, oy = lax.rem(z + dz, Z), lax.rem(y + dy, Y)
                at = pl.multiple_of(lax.rem(x + X - lax.rem(oz, X), X) * (Y * rows) + oy * rows, rows)
                block_here, block_there = mine_ref[pl.ds(at, rows), :], other_ref[pl.ds(at, rows), :]
                held[pl.ds((dy * Z + dz) * rows, rows), :] = jnp.where(lax.div(oz, X) == c, block_here, block_there)

    g = lax.dot_general(held[...], cot_ref[...], (((1,), (1,)), ((), ())), preferred_element_type=f32)
    part = rows // 2
    z_odd = lax.rem(here[0], 2) == 1

    def at_place(dy, dz, s):
        place = lambda dz: g[(dy * Z + dz) * rows + s * part :][:part]
        return place(dz) if s or dz in EVEN else jnp.where(z_odd, place((dz + Z - 2) % Z), place(dz))

    for out, places in zip(outs, UNITS):
        pieces = [at_place(*place) for place in places]
        if out.dtype == f32:
            for i, piece in enumerate(pieces):
                out[i * part : (i + 1) * part, :] = piece
        else:
            out[...] = jnp.concatenate(pieces, 0).astype(out.dtype)


EVEN, ODD = (0, 2, 4, 6), (1, 3, 5, 7)
UNITS = [[(dy, dz, 0) for dz in EVEN + ODD] for dy in (1, 3, 2)] + [[(dy, dz, 1) for dy in range(Y)] for dz in (4, 5)]
ROUNDED = len(UNITS)
UNITS += [[(0, dz, 0) for dz in EVEN + ODD]] + [[(dy, dz, 1) for dy in range(Y)] for dz in (3, 6, 2, 7, 1, 0)]


def gradient(mine, other, cotangent, here):
    half, tokens = mine.shape
    ff = cotangent.shape[1]
    part, tile = half // (Z * Y), min(1280, ff)
    whole = lambda i: (0, 0)
    shapes = [(len(places) * part, bf16 if k < ROUNDED else f32) for k, places in enumerate(UNITS)]
    cot = pltpu.with_memory_space_constraint(cotangent.T, pltpu.HBM)
    mine = pltpu.with_memory_space_constraint(mine, pltpu.HBM)
    other = pltpu.with_memory_space_constraint(other, pltpu.HBM)
    return pl.pallas_call(
        grad_kernel,
        grid=(pl.cdiv(ff, tile),),
        in_specs=[
            pl.BlockSpec(memory_space=pltpu.SMEM),
            pl.BlockSpec((half, tokens), whole),
            pl.BlockSpec((half, tokens), whole),
            pl.BlockSpec((tile, tokens), lambda i: (i, 0)),
        ],
        out_specs=[pl.BlockSpec((n, tile), lambda i: (0, i)) for n, _ in shapes],
        out_shape=[pltpu.HBM((n, ff), t) for n, t in shapes],
        scratch_shapes=[pltpu.VMEM((2 * half, tokens), bf16)],
        compiler_params=pltpu.CompilerParams(vmem_limit_bytes=24 * 2**20),
        cost_estimate=pl.CostEstimate(
            flops=4 * half * tokens * ff, bytes_accessed=2 * tokens * ff + 14 * half * ff // 2, transcendentals=0
        ),
    )(here, mine, other, cot)


def project(tokens, basis):
    c, x = lax.axis_index("c"), lax.axis_index("x")
    rank = basis.shape[1]
    half, part = rank // C, rank // (X * C)
    share = lambda k: lax.dot_general(
        lax.dynamic_slice_in_dim(basis, k * half, half, 1), tokens, (((0,), (1,)), ((), ())), preferred_element_type=f32
    )
    sent = moved(share(1 - c), "c", 1)
    both = share(c) + sent
    chunk = lambda d: lax.dynamic_slice_in_dim(both, (x + d) % X * part, part, 0)
    total = chunk(0)
    for got in [moved(chunk(d).astype(bf16), "x", d) for d in (1, 3, 2)]:
        total = total + got.astype(f32)
    mine = total.astype(bf16)
    got = {d: moved(mine, "x", d) for d in (1, 3, 2)}
    mine = jnp.concatenate([mine, got[1], got[2], got[3]], 0)
    return mine, moved(mine, "c", 1)


def scatter(one, three, two, four, five, zero, *rest):
    k3, k6, k2, k7, k1, k0 = rest
    up, down = moved(four, "z", 1), moved(five, "z", -1)
    across = [moved(one, "y", 1), moved(three, "y", 3), moved(two, "y", 2)]
    up = moved((k3 + up.astype(f32)).astype(bf16), "z", 1)
    down = moved((k6 + down.astype(f32)).astype(bf16), "z", -1)
    up, down = (k2 + up.astype(f32)).astype(bf16), (k7 + down.astype(f32)).astype(bf16)
    zero, up, down = lax.optimization_barrier((zero, up, down))
    up, down = moved(up, "z", 1), moved(down, "z", -1)
    h = zero.shape[0] // 2
    rows = h // 4
    high = zero[h:]
    for got in across:
        high = high + got[h:].astype(f32)
    pair = lax.ppermute(high.astype(bf16), "z", [(z, z ^ 1) for z in range(Z)])
    up = moved((k1 + up.astype(f32)).astype(bf16), "z", 1)
    low = zero[:h] + pair.astype(f32)
    for got in across:
        low = low + got[:h].astype(f32)
    first, low = low[:rows], low.astype(bf16)
    for k in (2, 1, 3):
        first = first + moved(low[k * rows : (k + 1) * rows], "z", 2 * k).astype(f32)
    second = k0 + up.astype(f32) + down.astype(f32)
    second, rounded = second[:rows], second.astype(bf16)
    for k in (2, 1, 3):
        second = second + moved(rounded[k * rows : (k + 1) * rows], "y", k).astype(f32)
    return jnp.concatenate([first, second], 0)


def picked(choices, index):
    out = choices[0]
    for k in range(1, len(choices)):
        out = jnp.where(index == k, choices[k], out)
    return out


def spread(normed, beside):
    z, y, x, c = (lax.axis_index(axis) for axis in ("z", "y", "x", "c"))
    rows, ff = normed.shape
    cut = normed.reshape(rows, Y, ff // Y).transpose(1, 0, 2)
    piece = lambda k: lax.dynamic_index_in_dim(cut, (y + k) % Y, 0, keepdims=False)
    got = {d: moved(piece(d), "y", d) for d in (1, 3, 2)}
    tall = jnp.stack([piece(0), got[1], got[2], got[3]])
    got = {d: moved(tall, "x", d) for d in (1, 3, 2)}
    wide = [tall, got[1], got[2], got[3]]
    odd = (z + c) % 2
    half = []
    for k in (0, 1, 2, 3):
        to = (z + 2 * k + odd) % Z
        sent = picked(wide, (x - to // 2) % X)
        pairs = []
        for pz in range(Z):
            for pc in range(C):
                po = (pz + pc) % 2
                for r in range(Y * X):
                    if k or po:
                        pairs.append(((pz * Y * X + r) * C + pc, (((pz + 2 * k + po) % Z) * Y * X + r) * C + (pc ^ po)))
        moved_in = lax.ppermute(sent, ("z", "y", "x", "c"), pairs)
        half.append(moved_in if k else jnp.where(odd == 0, sent, moved_in))
    half, beside = lax.optimization_barrier((jnp.stack(half), beside))
    return beside, half, moved(half, "c", 1)


def spread_order(rank):
    z, y, c = (lax.axis_index(axis) for axis in ("z", "y", "c"))
    rows = rank // (Z * Y)
    n = lax.broadcasted_iota(jnp.int32, (rank, rank), 1)
    r = lax.broadcasted_iota(jnp.int32, (rank, rank), 0)
    h, k, j = n // (rank // 2), (n // (rows * Y)) % (Z // 2), (n // rows) % Y
    owner_z = (z + 2 * Z - 2 * k - (z + c + h) % 2) % Z
    want = (owner_z * Y + (y + Y - j) % Y) * rows + n % rows
    return (r == want).astype(bf16)


def shards(tokens, basis, cotangent, exp_avg, exp_avg_sq):
    rank, ff = basis.shape[1], cotangent.shape[1]
    here = jnp.stack([lax.axis_index(axis) for axis in ("z", "y", "x", "c")]).astype(jnp.int32)
    mine, other = project(tokens, basis)
    units = gradient(mine, other, cotangent, here)
    total = scatter(*units)
    total_tokens = cotangent.shape[0] * Z * Y
    grad_low = total * (1.0 / total_tokens)
    first = 0.9 * exp_avg + 0.1 * grad_low
    second = 0.999 * exp_avg_sq + 0.001 * grad_low * grad_low
    normed = (first / bias_first / (jnp.sqrt(second / bias_second) + 1e-08)).astype(bf16)
    ordered = jnp.dot(basis, spread_order(rank), preferred_element_type=f32).astype(bf16)
    ordered, *parts = spread(normed, ordered)
    mine, other = (part.reshape(rank // 2, ff // Y) for part in parts)
    update = jnp.dot(ordered[:, : rank // 2], mine, preferred_element_type=f32)
    update = (update + jnp.dot(ordered[:, rank // 2 :], other, preferred_element_type=f32)).astype(bf16)
    return (update, first, second)


def solution(mesh):
    fine = Mesh(np.asarray(mesh.devices).reshape(Z, Y, X, C), ("z", "y", "x", "c"))
    dp, fsdp = ("z", "y"), ("x", "c")
    in_specs = (P(dp, fsdp), P(fsdp, None), P(dp, fsdp), P(dp, fsdp), P(dp, fsdp))
    out_specs = (P(fsdp, dp), P(dp, fsdp), P(dp, fsdp))
    return jax.shard_map(shards, mesh=fine, in_specs=in_specs, out_specs=out_specs, check_vma=False)
```

```python
import functools

import numpy as np
import jax
import jax.numpy as jnp
from jax import lax
from jax.experimental import pallas as pl
from jax.experimental.pallas import tpu as pltpu
from jax.sharding import Mesh, PartitionSpec as P

bias_first = 1.0 - 0.9**10
bias_second = 1.0 - 0.999**10
Z, Y, X, C = 8, 4, 4, 2
f32, bf16 = jnp.float32, jnp.bfloat16


def moved(value, axis, by):
    n = {"z": Z, "y": Y, "x": X, "c": C}[axis]
    return lax.ppermute(value, axis, [(i, (i + by) % n) for i in range(n)])


EVEN, ODD = (0, 2, 4, 6), (1, 3, 5, 7)
Y_FIRST = [[(dy, dz) for dz in half] for dy in (2, 1, 3, 0) for half in (EVEN, ODD)]
Z_FIRST = [[(dy, dz) for dy in range(Y)] for dz in (4, 5, 3, 6, 2, 7, 1, 0)]


def grad_kernel(units, here, mine_ref, other_ref, cot_ref, *rest):
    outs, held = rest[:-1], rest[-1]
    rows = held.shape[0] // (Z * Y)
    z_odd = lax.rem(here[0], 2) == 1

    @pl.when(pl.program_id(0) == 0)
    def _():
        z, y, x, c = (here[i] for i in range(4))
        for dy in range(Y):
            for dz in range(Z):
                oz, oy = lax.rem(z + dz, Z), lax.rem(y + dy, Y)
                at = pl.multiple_of(lax.rem(x + X - lax.rem(oz, X), X) * (Y * rows) + oy * rows, rows)
                block_here, block_there = mine_ref[pl.ds(at, rows), :], other_ref[pl.ds(at, rows), :]
                held[pl.ds((dy * Z + dz) * rows, rows), :] = jnp.where(lax.div(oz, X) == c, block_here, block_there)

    g = lax.dot_general(held[...], cot_ref[...], (((1,), (1,)), ((), ())), preferred_element_type=f32)
    place = lambda dy, dz: g[(dy * Z + dz % Z) * rows :][:rows]
    for out, places in zip(outs, units):
        turn = units is Y_FIRST and places[0][1] in ODD
        for i, (dy, dz) in enumerate(places):
            piece = jnp.where(z_odd, place(dy, dz - 2), place(dy, dz)) if turn else place(dy, dz)
            out[i * rows : (i + 1) * rows, :] = piece.astype(out.dtype)


def gradient(units, mine, other, cotangent, here, tile, start, stop):
    half, tokens = mine.shape
    ff = min(stop * tile, cotangent.shape[1]) - start * tile
    rows = 2 * half // (Z * Y)
    whole = lambda i: (0, 0)
    shapes = [(len(places) * rows, f32 if k > 1 else bf16) for k, places in enumerate(units)]
    return pl.pallas_call(
        functools.partial(grad_kernel, units),
        grid=(stop - start,),
        in_specs=[
            pl.BlockSpec(memory_space=pltpu.SMEM),
            pl.BlockSpec((half, tokens), whole),
            pl.BlockSpec((half, tokens), whole),
            pl.BlockSpec((tile, tokens), lambda i: (start + i, 0)),
        ],
        out_specs=[pl.BlockSpec((n, tile), lambda i: (0, i)) for n, _ in shapes],
        out_shape=[pltpu.HBM((n, ff), t) for n, t in shapes],
        scratch_shapes=[pltpu.VMEM((2 * half, tokens), bf16)],
        compiler_params=pltpu.CompilerParams(vmem_limit_bytes=20 * 2**20),
        cost_estimate=pl.CostEstimate(
            flops=4 * half * tokens * ff, bytes_accessed=2 * tokens * ff + 14 * half * ff // 2, transcendentals=0
        ),
    )(here, *(pltpu.with_memory_space_constraint(v, pltpu.HBM) for v in (mine, other, cotangent.T)))


def near_order(rank):
    c, x = lax.axis_index("c"), lax.axis_index("x")
    part = rank // (X * C)
    n = lax.broadcasted_iota(jnp.int32, (rank, rank), 0)
    r = lax.broadcasted_iota(jnp.int32, (rank, rank), 1)
    chunk = ((c + n // (part * X)) % C) * X + (x + (n // part) % X) % X
    return (r == chunk * part + n % part).astype(bf16)


def project(tokens, basis, beside):
    rank = basis.shape[1]
    half, part = rank // C, rank // (X * C)
    lanes = (((1,), (1,)), ((), ()))
    ordered = lax.dot_general(near_order(rank), basis, lanes, preferred_element_type=f32).astype(bf16)
    away = lax.dot_general(ordered[half:], tokens, lanes, preferred_element_type=f32)
    sent = moved(away, "c", 1)
    both = lax.dot_general(ordered[:half], tokens, lanes, preferred_element_type=f32) + sent
    total = both[:part]
    for got in [moved(both[d * part : (d + 1) * part].astype(bf16), "x", d) for d in (1, 3, 2)]:
        total = total + got.astype(f32)
    mine = total.astype(bf16)
    got = {d: moved(mine, "x", d) for d in (1, 3, 2)}
    mine, beside = lax.optimization_barrier((jnp.concatenate([mine, got[1], got[2], got[3]], 0), beside))
    return mine, moved(mine, "c", 1), beside


def scatter(ring, relay):
    four, five, k3, k6, k2, k7, k1, k0 = ring()
    up, down = moved(four, "z", 1), moved(five, "z", -1)
    two_low, two_high, one_low, one_high, three_low, three_high, low, high = relay()
    high_y, low_y = moved(two_low, "y", 1), moved(two_high, "y", -1)
    up = moved((k3 + up.astype(f32)).astype(bf16), "z", 1)
    down = moved((k6 + down.astype(f32)).astype(bf16), "z", -1)
    one = jnp.concatenate([(one_low + high_y.astype(f32)).astype(bf16), one_high.astype(bf16)], 0)
    three = jnp.concatenate([three_low.astype(bf16), (three_high + low_y.astype(f32)).astype(bf16)], 0)
    across = [moved(one, "y", 1), moved(three, "y", -1)]
    up, down = (k2 + up.astype(f32)).astype(bf16), (k7 + down.astype(f32)).astype(bf16)
    up, down = moved(up, "z", 1), moved(down, "z", -1)
    h = low.shape[0]
    rows = h // 4
    for got in across:
        high = high + got[h:].astype(f32)
    pair = lax.ppermute(high.astype(bf16), "z", [(z, z ^ 1) for z in range(Z)])
    up = moved((k1 + up.astype(f32)).astype(bf16), "z", 1)
    low = low + pair.astype(f32)
    for got in across:
        low = low + got[:h].astype(f32)
    first, low = low[:rows], low.astype(bf16)
    for k in (2, 1, 3):
        first = first + moved(low[k * rows : (k + 1) * rows], "z", 2 * k).astype(f32)
    second = k0 + up.astype(f32) + down.astype(f32)
    second, rounded = second[:rows], second.astype(bf16)
    for k in (2, 1, 3):
        second = second + moved(rounded[k * rows : (k + 1) * rows], "y", k).astype(f32)
    return jnp.concatenate([first, second], 1)


def picked(choices, index):
    out = choices[0]
    for k in range(1, len(choices)):
        out = jnp.where(index == k, choices[k], out)
    return out


def spread(normed):
    z, y, x, c = (lax.axis_index(axis) for axis in ("z", "y", "x", "c"))
    rows, ff = normed.shape
    cut = normed.reshape(rows, Y, ff // Y).transpose(1, 0, 2)
    piece = lambda k: lax.dynamic_index_in_dim(cut, (y + k) % Y, 0, keepdims=False)
    got = {d: moved(piece(d), "y", d) for d in (1, 3, 2)}
    tall = jnp.stack([piece(0), got[1], got[2], got[3]])
    got = {d: moved(tall, "x", d) for d in (1, 3, 2)}
    wide = [tall, got[1], got[2], got[3]]
    odd = (z + c) % 2
    half = []
    for k in range(Z // 2):
        to = (z + 2 * k + odd) % Z
        sent = picked(wide, (x - to // 2) % X)
        pairs = []
        for pz in range(Z):
            for pc in range(C):
                po = (pz + pc) % 2
                for r in range(Y * X):
                    if k or po:
                        pairs.append(((pz * Y * X + r) * C + pc, (((pz + 2 * k + po) % Z) * Y * X + r) * C + (pc ^ po)))
        moved_in = lax.ppermute(sent, ("z", "y", "x", "c"), pairs)
        half.append(moved_in if k else jnp.where(odd == 0, sent, moved_in))
    half = jnp.stack(half)
    return half, moved(half, "c", 1)


def spread_order(rank):
    z, y, c = (lax.axis_index(axis) for axis in ("z", "y", "c"))
    rows = rank // (Z * Y)
    n = lax.broadcasted_iota(jnp.int32, (rank, rank), 1)
    r = lax.broadcasted_iota(jnp.int32, (rank, rank), 0)
    h, k, j = n // (rank // 2), (n // (rows * Y)) % (Z // 2), (n // rows) % Y
    owner_z = (z + 2 * Z - 2 * k - (z + c + h) % 2) % Z
    want = (owner_z * Y + (y + Y - j) % Y) * rows + n % rows
    return (r == want).astype(bf16)


def shards(tokens, basis, cotangent, exp_avg, exp_avg_sq):
    rank, ff = basis.shape[1], cotangent.shape[1]
    here = jnp.stack([lax.axis_index(axis) for axis in ("z", "y", "x", "c")]).astype(jnp.int32)
    ordered = jnp.dot(basis, spread_order(rank), preferred_element_type=f32).astype(bf16)
    mine, other, ordered = project(tokens, basis, ordered)
    lanes = 128
    tile = pl.cdiv(pl.cdiv(ff, lanes), 6) * lanes
    tiles = pl.cdiv(ff, tile)
    made = functools.partial(gradient, mine=mine, other=other, cotangent=cotangent, here=here, tile=tile)
    total = scatter(
        lambda: made(Z_FIRST, start=tiles // 2, stop=tiles), lambda: made(Y_FIRST, start=0, stop=tiles // 2)
    )
    total_tokens = cotangent.shape[0] * Z * Y
    grad_low = total * (1.0 / total_tokens)
    first = 0.9 * exp_avg + 0.1 * grad_low
    second = 0.999 * exp_avg_sq + 0.001 * grad_low * grad_low
    normed = (first / bias_first / (jnp.sqrt(second / bias_second) + 1e-08)).astype(bf16)
    mine, other = (part.reshape(rank // 2, ff // Y) for part in spread(normed))
    update = jnp.dot(ordered[:, : rank // 2], mine, preferred_element_type=f32)
    update = (update + jnp.dot(ordered[:, rank // 2 :], other, preferred_element_type=f32)).astype(bf16)
    return (update, first, second)


def solution(mesh):
    fine = Mesh(np.asarray(mesh.devices).reshape(Z, Y, X, C), ("z", "y", "x", "c"))
    dp, fsdp = ("z", "y"), ("x", "c")
    in_specs = (P(dp, fsdp), P(fsdp, None), P(dp, fsdp), P(dp, fsdp), P(dp, fsdp))
    out_specs = (P(fsdp, dp), P(dp, fsdp), P(dp, fsdp))
    return jax.shard_map(shards, mesh=fine, in_specs=in_specs, out_specs=out_specs, check_vma=False)
```

```python
import numpy as np
import jax
import jax.numpy as jnp
from jax import lax
from jax.experimental import pallas as pl
from jax.experimental.pallas import tpu as pltpu
from jax.sharding import Mesh, PartitionSpec as P

bias_first = 1.0 - 0.9**10
bias_second = 1.0 - 0.999**10
Z, Y, X, C = 8, 4, 4, 2
f32, bf16 = jnp.float32, jnp.bfloat16


def moved(value, axis, by):
    n = {"z": Z, "y": Y, "x": X, "c": C}[axis]
    return lax.ppermute(value, axis, [(i, (i + by) % n) for i in range(n)])


EVEN, ODD = (0, 2, 4, 6), (1, 3, 5, 7)
UNITS = [[(dy, dz, 0) for dz in half] for dy in (2, 1, 3, 0) for half in (EVEN, ODD)]
UNITS += [[(dy, dz, 1) for dy in range(Y)] for dz in (4, 5, 3, 6, 2, 7, 1, 0)]
ROUNDED = (0, 1, 3, 4, 8, 9)


def grad_kernel(here, mine_ref, other_ref, cot_ref, *rest):
    outs, held = rest[:-1], rest[-1]
    rows = held.shape[0] // (Z * Y)
    part = rows // 2
    z_odd = lax.rem(here[0], 2) == 1

    @pl.when(pl.program_id(0) == 0)
    def _():
        z, y, x, c = (here[i] for i in range(4))
        for dy in range(Y):
            for dz in range(Z):
                oz, oy = lax.rem(z + dz, Z), lax.rem(y + dy, Y)
                at = pl.multiple_of(lax.rem(x + X - lax.rem(oz, X), X) * (Y * rows) + oy * rows, rows)
                block_here, block_there = mine_ref[pl.ds(at, rows), :], other_ref[pl.ds(at, rows), :]
                held[pl.ds((dy * Z + dz) * rows, rows), :] = jnp.where(lax.div(oz, X) == c, block_here, block_there)

    g = lax.dot_general(held[...], cot_ref[...], (((1,), (1,)), ((), ())), preferred_element_type=f32)

    def place(dy, dz, s):
        block = lambda dz: g[(dy * Z + dz % Z) * rows + s * part :][:part]
        return jnp.where(z_odd, block(dz - 2), block(dz)) if s == 0 and dz in ODD else block(dz)

    for out, places in zip(outs, UNITS):
        pieces = [place(*at) for at in places]
        if out.dtype == f32:
            for i, piece in enumerate(pieces):
                out[i * part : (i + 1) * part, :] = piece
        else:
            out[...] = jnp.concatenate(pieces, 0).astype(out.dtype)


def gradient(mine, other, cotangent, here):
    half, tokens = mine.shape
    ff = cotangent.shape[1]
    part, tile = half // (Z * Y), min(1280, ff)
    whole = lambda i: (0, 0)
    shapes = [(len(places) * part, bf16 if k in ROUNDED else f32) for k, places in enumerate(UNITS)]
    held_in = pltpu.with_memory_space_constraint
    return pl.pallas_call(
        grad_kernel,
        grid=(pl.cdiv(ff, tile),),
        in_specs=[
            pl.BlockSpec(memory_space=pltpu.SMEM),
            pl.BlockSpec(memory_space=pltpu.VMEM),
            pl.BlockSpec(memory_space=pltpu.VMEM),
            pl.BlockSpec((tile, tokens), lambda i: (i, 0)),
        ],
        out_specs=[pl.BlockSpec((n, tile), lambda i: (0, i)) for n, _ in shapes],
        out_shape=[pltpu.HBM((n, ff), t) for n, t in shapes],
        scratch_shapes=[pltpu.VMEM((2 * half, tokens), bf16)],
        compiler_params=pltpu.CompilerParams(vmem_limit_bytes=24 * 2**20),
        cost_estimate=pl.CostEstimate(
            flops=4 * half * tokens * ff, bytes_accessed=2 * tokens * ff + 14 * half * ff // 2, transcendentals=0
        ),
    )(here, held_in(mine, pltpu.VMEM), held_in(other, pltpu.VMEM), held_in(cotangent.T, pltpu.HBM))


def near_order(rank):
    c, x = lax.axis_index("c"), lax.axis_index("x")
    part = rank // (X * C)
    n = lax.broadcasted_iota(jnp.int32, (rank, rank), 0)
    r = lax.broadcasted_iota(jnp.int32, (rank, rank), 1)
    chunk = ((c + n // (part * X)) % C) * X + (x + (n // part) % X) % X
    return (r == chunk * part + n % part).astype(bf16)


def project(tokens, basis, beside):
    rank = basis.shape[1]
    half, part = rank // C, rank // (X * C)
    lanes = (((1,), (1,)), ((), ()))
    ordered = lax.dot_general(near_order(rank), basis, lanes, preferred_element_type=f32).astype(bf16)
    away = lax.dot_general(ordered[half:], tokens, lanes, preferred_element_type=f32)
    sent = moved(away, "c", 1)
    both = lax.dot_general(ordered[:half], tokens, lanes, preferred_element_type=f32) + sent
    total = both[:part]
    for got in [moved(both[d * part : (d + 1) * part].astype(bf16), "x", d) for d in (1, 3, 2)]:
        total = total + got.astype(f32)
    mine = total.astype(bf16)
    got = {d: moved(mine, "x", d) for d in (1, 3, 2)}
    mine, beside = lax.optimization_barrier((jnp.concatenate([mine, got[1], got[2], got[3]], 0), beside))
    return mine, moved(mine, "c", 1), beside


def scatter(*units):
    two_low, two_high, one_low, one_high, three_low, three_high, low, high = units[:8]
    four, five, k3, k6, k2, k7, k1, k0 = units[8:]
    up, down = moved(four, "z", 1), moved(five, "z", -1)
    high_y, low_y = moved(two_low, "y", 1), moved(two_high, "y", -1)
    up = moved((k3 + up.astype(f32)).astype(bf16), "z", 1)
    down = moved((k6 + down.astype(f32)).astype(bf16), "z", -1)
    one = jnp.concatenate([(one_low + high_y.astype(f32)).astype(bf16), one_high], 0)
    three = jnp.concatenate([three_low, (three_high + low_y.astype(f32)).astype(bf16)], 0)
    across = [moved(one, "y", 1), moved(three, "y", -1)]
    up, down = (k2 + up.astype(f32)).astype(bf16), (k7 + down.astype(f32)).astype(bf16)
    up, down = moved(up, "z", 1), moved(down, "z", -1)
    h = low.shape[0]
    rows = h // 4
    for got in across:
        high = high + got[h:].astype(f32)
    pair = lax.ppermute(high.astype(bf16), "z", [(z, z ^ 1) for z in range(Z)])
    up = moved((k1 + up.astype(f32)).astype(bf16), "z", 1)
    low = low + pair.astype(f32)
    for got in across:
        low = low + got[:h].astype(f32)
    first, low = low[:rows], low.astype(bf16)
    for k in (2, 1, 3):
        first = first + moved(low[k * rows : (k + 1) * rows], "z", 2 * k).astype(f32)
    second = k0 + up.astype(f32) + down.astype(f32)
    second, rounded = second[:rows], second.astype(bf16)
    for k in (2, 1, 3):
        second = second + moved(rounded[k * rows : (k + 1) * rows], "y", k).astype(f32)
    return jnp.concatenate([first, second], 0)


def picked(choices, index):
    out = choices[0]
    for k in range(1, len(choices)):
        out = jnp.where(index == k, choices[k], out)
    return out


def spread(normed):
    z, y, x, c = (lax.axis_index(axis) for axis in ("z", "y", "x", "c"))
    rows, ff = normed.shape
    cut = normed.reshape(rows, Y, ff // Y).transpose(1, 0, 2)
    piece = lambda k: lax.dynamic_index_in_dim(cut, (y + k) % Y, 0, keepdims=False)
    got = {d: moved(piece(d), "y", d) for d in (1, 3, 2)}
    tall = jnp.stack([piece(0), got[1], got[2], got[3]])
    got = {d: moved(tall, "x", d) for d in (1, 3, 2)}
    wide = [tall, got[1], got[2], got[3]]
    odd = (z + c) % 2
    half = []
    for k in range(Z // 2):
        to = (z + 2 * k + odd) % Z
        sent = picked(wide, (x - to // 2) % X)
        pairs = []
        for pz in range(Z):
            for pc in range(C):
                po = (pz + pc) % 2
                for r in range(Y * X):
                    if k or po:
                        pairs.append(((pz * Y * X + r) * C + pc, (((pz + 2 * k + po) % Z) * Y * X + r) * C + (pc ^ po)))
        moved_in = lax.ppermute(sent, ("z", "y", "x", "c"), pairs)
        half.append(moved_in if k else jnp.where(odd == 0, sent, moved_in))
    half = jnp.stack(half)
    return half, moved(half, "c", 1)


def spread_order(rank):
    z, y, c = (lax.axis_index(axis) for axis in ("z", "y", "c"))
    rows = rank // (Z * Y)
    n = lax.broadcasted_iota(jnp.int32, (rank, rank), 1)
    r = lax.broadcasted_iota(jnp.int32, (rank, rank), 0)
    h, k, j = n // (rank // 2), (n // (rows * Y)) % (Z // 2), (n // rows) % Y
    owner_z = (z + 2 * Z - 2 * k - (z + c + h) % 2) % Z
    want = (owner_z * Y + (y + Y - j) % Y) * rows + n % rows
    return (r == want).astype(bf16)


def shards(tokens, basis, cotangent, exp_avg, exp_avg_sq):
    rank, ff = basis.shape[1], cotangent.shape[1]
    here = jnp.stack([lax.axis_index(axis) for axis in ("z", "y", "x", "c")]).astype(jnp.int32)
    ordered = jnp.dot(basis, spread_order(rank), preferred_element_type=f32).astype(bf16)
    mine, other, ordered = project(tokens, basis, ordered)
    total = scatter(*gradient(mine, other, cotangent, here))
    total_tokens = cotangent.shape[0] * Z * Y
    grad_low = total * (1.0 / total_tokens)
    first = 0.9 * exp_avg + 0.1 * grad_low
    second = 0.999 * exp_avg_sq + 0.001 * grad_low * grad_low
    normed = (first / bias_first / (jnp.sqrt(second / bias_second) + 1e-08)).astype(bf16)
    mine, other = (part.reshape(rank // 2, ff // Y) for part in spread(normed))
    update = jnp.dot(ordered[:, : rank // 2], mine, preferred_element_type=f32)
    update = (update + jnp.dot(ordered[:, rank // 2 :], other, preferred_element_type=f32)).astype(bf16)
    return (update, first, second)


def solution(mesh):
    fine = Mesh(np.asarray(mesh.devices).reshape(Z, Y, X, C), ("z", "y", "x", "c"))
    dp, fsdp = ("z", "y"), ("x", "c")
    in_specs = (P(dp, fsdp), P(fsdp, None), P(dp, fsdp), P(dp, fsdp), P(dp, fsdp))
    out_specs = (P(fsdp, dp), P(dp, fsdp), P(dp, fsdp))
    return jax.shard_map(shards, mesh=fine, in_specs=in_specs, out_specs=out_specs, check_vma=False)
```

```python
import functools

import numpy as np
import jax
import jax.numpy as jnp
from jax import lax
from jax.experimental import pallas as pl
from jax.experimental.pallas import tpu as pltpu
from jax.sharding import Mesh, PartitionSpec as P

bias_first = 1.0 - 0.9**10
bias_second = 1.0 - 0.999**10
Z, Y, X, C = 8, 4, 4, 2
f32, bf16 = jnp.float32, jnp.bfloat16


def moved(value, axis, by):
    n = {"z": Z, "y": Y, "x": X, "c": C}[axis]
    return lax.ppermute(value, axis, [(i, (i + by) % n) for i in range(n)])


EVEN, ODD = (0, 2, 4, 6), (1, 3, 5, 7)
Y_FIRST = [[(dy, dz) for dz in half] for dy in (2, 1, 3, 0) for half in (EVEN, ODD)]
Z_FIRST = [[(dy, dz) for dy in range(Y)] for dz in (4, 5, 3, 6, 2, 7, 1, 0)]
Y_ROUNDED, Z_ROUNDED = (0, 1, 3, 4), (0, 1)


def grad_kernel(units, here, mine_ref, other_ref, cot_ref, *rest):
    outs, held = rest[:-1], rest[-1]
    rows = held.shape[0] // (Z * Y)
    z_odd = lax.rem(here[0], 2) == 1

    @pl.when(pl.program_id(0) == 0)
    def _():
        z, y, x, c = (here[i] for i in range(4))
        for dy in range(Y):
            for dz in range(Z):
                oz, oy = lax.rem(z + dz, Z), lax.rem(y + dy, Y)
                at = pl.multiple_of(lax.rem(x + X - lax.rem(oz, X), X) * (Y * rows) + oy * rows, rows)
                block_here, block_there = mine_ref[pl.ds(at, rows), :], other_ref[pl.ds(at, rows), :]
                held[pl.ds((dy * Z + dz) * rows, rows), :] = jnp.where(lax.div(oz, X) == c, block_here, block_there)

    g = lax.dot_general(held[...], cot_ref[...], (((1,), (1,)), ((), ())), preferred_element_type=f32)
    place = lambda dy, dz: g[(dy * Z + dz % Z) * rows :][:rows]
    for out, places in zip(outs, units):
        turn = units is Y_FIRST and places[0][1] in ODD
        for i, (dy, dz) in enumerate(places):
            piece = jnp.where(z_odd, place(dy, dz - 2), place(dy, dz)) if turn else place(dy, dz)
            out[i * rows : (i + 1) * rows, :] = piece.astype(out.dtype)


def gradient(units, mine, other, cotangent, here, tile, start, stop):
    half, tokens = mine.shape
    ff = min(stop * tile, cotangent.shape[1]) - start * tile
    rows = 2 * half // (Z * Y)
    shapes = [(len(places) * rows, bf16 if k in (Y_ROUNDED if units is Y_FIRST else Z_ROUNDED) else f32) for k, places in enumerate(units)]
    held_in = pltpu.with_memory_space_constraint
    return pl.pallas_call(
        functools.partial(grad_kernel, units),
        grid=(stop - start,),
        in_specs=[
            pl.BlockSpec(memory_space=pltpu.SMEM),
            pl.BlockSpec(memory_space=pltpu.VMEM),
            pl.BlockSpec(memory_space=pltpu.VMEM),
            pl.BlockSpec((tile, tokens), lambda i: (start + i, 0)),
        ],
        out_specs=[pl.BlockSpec((n, tile), lambda i: (0, i)) for n, _ in shapes],
        out_shape=[pltpu.HBM((n, ff), t) for n, t in shapes],
        scratch_shapes=[pltpu.VMEM((2 * half, tokens), bf16)],
        compiler_params=pltpu.CompilerParams(vmem_limit_bytes=20 * 2**20),
        cost_estimate=pl.CostEstimate(
            flops=4 * half * tokens * ff, bytes_accessed=2 * tokens * ff + 14 * half * ff // 2, transcendentals=0
        ),
    )(here, held_in(mine, pltpu.VMEM), held_in(other, pltpu.VMEM), held_in(cotangent.T, pltpu.HBM))


def near_order(rank):
    c, x = lax.axis_index("c"), lax.axis_index("x")
    part = rank // (X * C)
    n = lax.broadcasted_iota(jnp.int32, (rank, rank), 0)
    r = lax.broadcasted_iota(jnp.int32, (rank, rank), 1)
    chunk = ((c + n // (part * X)) % C) * X + (x + (n // part) % X) % X
    return (r == chunk * part + n % part).astype(bf16)


def project(tokens, basis, beside):
    rank = basis.shape[1]
    half, part = rank // C, rank // (X * C)
    lanes = (((1,), (1,)), ((), ()))
    ordered = lax.dot_general(near_order(rank), basis, lanes, preferred_element_type=f32).astype(bf16)
    away = lax.dot_general(ordered[half:], tokens, lanes, preferred_element_type=f32)
    sent = moved(away, "c", 1)
    both = lax.dot_general(ordered[:half], tokens, lanes, preferred_element_type=f32) + sent
    total = both[:part]
    for got in [moved(both[d * part : (d + 1) * part].astype(bf16), "x", d) for d in (1, 3, 2)]:
        total = total + got.astype(f32)
    mine = total.astype(bf16)
    got = {d: moved(mine, "x", d) for d in (1, 3, 2)}
    mine, beside = lax.optimization_barrier((jnp.concatenate([mine, got[1], got[2], got[3]], 0), beside))
    return mine, moved(mine, "c", 1), beside


def scatter(ring, relay):
    four, five, k3, k6, k2, k7, k1, k0 = ring()
    up, down = moved(four, "z", 1), moved(five, "z", -1)
    two_low, two_high, one_low, one_high, three_low, three_high, low, high = relay()
    high_y, low_y = moved(two_low, "y", 1), moved(two_high, "y", -1)
    up = moved((k3 + up.astype(f32)).astype(bf16), "z", 1)
    down = moved((k6 + down.astype(f32)).astype(bf16), "z", -1)
    one = jnp.concatenate([(one_low + high_y.astype(f32)).astype(bf16), one_high], 0)
    three = jnp.concatenate([three_low, (three_high + low_y.astype(f32)).astype(bf16)], 0)
    across = [moved(one, "y", 1), moved(three, "y", -1)]
    up, down = (k2 + up.astype(f32)).astype(bf16), (k7 + down.astype(f32)).astype(bf16)
    up, down = moved(up, "z", 1), moved(down, "z", -1)
    h = low.shape[0]
    rows = h // 4
    for got in across:
        high = high + got[h:].astype(f32)
    pair = lax.ppermute(high.astype(bf16), "z", [(z, z ^ 1) for z in range(Z)])
    up = moved((k1 + up.astype(f32)).astype(bf16), "z", 1)
    low = low + pair.astype(f32)
    for got in across:
        low = low + got[:h].astype(f32)
    first, low = low[:rows], low.astype(bf16)
    for k in (2, 1, 3):
        first = first + moved(low[k * rows : (k + 1) * rows], "z", 2 * k).astype(f32)
    second = k0 + up.astype(f32) + down.astype(f32)
    second, rounded = second[:rows], second.astype(bf16)
    for k in (2, 1, 3):
        second = second + moved(rounded[k * rows : (k + 1) * rows], "y", k).astype(f32)
    return jnp.concatenate([first, second], 1)


def picked(choices, index):
    out = choices[0]
    for k in range(1, len(choices)):
        out = jnp.where(index == k, choices[k], out)
    return out


def spread(normed, beside):
    z, y, x, c = (lax.axis_index(axis) for axis in ("z", "y", "x", "c"))
    rows, ff = normed.shape
    cut = normed.reshape(rows, Y, ff // Y).transpose(1, 0, 2)
    piece = lambda k: lax.dynamic_index_in_dim(cut, (y + k) % Y, 0, keepdims=False)
    got = {d: moved(piece(d), "y", d) for d in (1, 3, 2)}
    tall = jnp.stack([piece(0), got[1], got[2], got[3]])
    got = {d: moved(tall, "x", d) for d in (1, 3, 2)}
    wide = [tall, got[1], got[2], got[3]]
    odd = (z + c) % 2
    half = []
    for k in range(Z // 2):
        to = (z + 2 * k + odd) % Z
        sent = picked(wide, (x - to // 2) % X)
        pairs = []
        for pz in range(Z):
            for pc in range(C):
                po = (pz + pc) % 2
                for r in range(Y * X):
                    if k or po:
                        pairs.append(((pz * Y * X + r) * C + pc, (((pz + 2 * k + po) % Z) * Y * X + r) * C + (pc ^ po)))
        moved_in = lax.ppermute(sent, ("z", "y", "x", "c"), pairs)
        half.append(moved_in if k else jnp.where(odd == 0, sent, moved_in))
    half, beside = lax.optimization_barrier((jnp.stack(half), beside))
    return beside, half, moved(half, "c", 1)


def spread_order(rank):
    z, y, c = (lax.axis_index(axis) for axis in ("z", "y", "c"))
    rows = rank // (Z * Y)
    n = lax.broadcasted_iota(jnp.int32, (rank, rank), 1)
    r = lax.broadcasted_iota(jnp.int32, (rank, rank), 0)
    h, k, j = n // (rank // 2), (n // (rows * Y)) % (Z // 2), (n // rows) % Y
    owner_z = (z + 2 * Z - 2 * k - (z + c + h) % 2) % Z
    want = (owner_z * Y + (y + Y - j) % Y) * rows + n % rows
    return (r == want).astype(bf16)


def shards(tokens, basis, cotangent, exp_avg, exp_avg_sq):
    rank, ff = basis.shape[1], cotangent.shape[1]
    here = jnp.stack([lax.axis_index(axis) for axis in ("z", "y", "x", "c")]).astype(jnp.int32)
    ordered = jnp.dot(basis, spread_order(rank), preferred_element_type=f32).astype(bf16)
    mine, other, ordered = project(tokens, basis, ordered)
    lanes = 128
    tile = pl.cdiv(pl.cdiv(ff, lanes), 6) * lanes
    tiles = pl.cdiv(ff, tile)
    made = functools.partial(gradient, mine=mine, other=other, cotangent=cotangent, here=here, tile=tile)
    relay = functools.partial(made, Y_FIRST, start=0, stop=tiles // 2)
    total = scatter(functools.partial(made, Z_FIRST, start=tiles // 2, stop=tiles), relay)
    total_tokens = cotangent.shape[0] * Z * Y
    grad_low = total * (1.0 / total_tokens)
    first = 0.9 * exp_avg + 0.1 * grad_low
    second = 0.999 * exp_avg_sq + 0.001 * grad_low * grad_low
    normed = (first / bias_first / (jnp.sqrt(second / bias_second) + 1e-08)).astype(bf16)
    ordered, *parts = spread(normed, ordered)
    mine, other = (part.reshape(rank // 2, ff // Y) for part in parts)
    update = jnp.dot(ordered[:, : rank // 2], mine, preferred_element_type=f32)
    update = (update + jnp.dot(ordered[:, rank // 2 :], other, preferred_element_type=f32)).astype(bf16)
    return (update, first, second)


def solution(mesh):
    fine = Mesh(np.asarray(mesh.devices).reshape(Z, Y, X, C), ("z", "y", "x", "c"))
    dp, fsdp = ("z", "y"), ("x", "c")
    in_specs = (P(dp, fsdp), P(fsdp, None), P(dp, fsdp), P(dp, fsdp), P(dp, fsdp))
    out_specs = (P(fsdp, dp), P(dp, fsdp), P(dp, fsdp))
    return jax.shard_map(shards, mesh=fine, in_specs=in_specs, out_specs=out_specs, check_vma=False)
```

```python
import functools

import numpy as np
import jax
import jax.numpy as jnp
from jax import lax
from jax.experimental import pallas as pl
from jax.experimental.pallas import tpu as pltpu
from jax.sharding import Mesh, PartitionSpec as P

bias_first = 1.0 - 0.9**10
bias_second = 1.0 - 0.999**10
Z, Y, X, C = 8, 4, 4, 2
f32, bf16 = jnp.float32, jnp.bfloat16


def moved(value, axis, by):
    n = {"z": Z, "y": Y, "x": X, "c": C}[axis]
    return lax.ppermute(value, axis, [(i, (i + by) % n) for i in range(n)])


EVEN, ODD = (0, 2, 4, 6), (1, 3, 5, 7)
Y_FIRST = [[(dy, dz) for dz in half] for dy in (2, 1, 3, 0) for half in (EVEN, ODD)]
Z_FIRST = [[(dy, dz) for dy in range(Y)] for dz in (4, 5, 3, 6, 2, 7, 1, 0)]
Y_ROUNDED, Z_ROUNDED = (0, 1, 3, 4), (0, 1)


def grad_kernel(units, here, mine_ref, other_ref, cot_ref, *rest):
    outs, held = rest[:-1], rest[-1]
    rows = held.shape[0] // (Z * Y)
    z_odd = lax.rem(here[0], 2) == 1

    @pl.when(pl.program_id(0) == 0)
    def _():
        z, y, x, c = (here[i] for i in range(4))
        for dy in range(Y):
            for dz in range(Z):
                oz, oy = lax.rem(z + dz, Z), lax.rem(y + dy, Y)
                at = pl.multiple_of(lax.rem(x + X - lax.rem(oz, X), X) * (Y * rows) + oy * rows, rows)
                block_here, block_there = mine_ref[pl.ds(at, rows), :], other_ref[pl.ds(at, rows), :]
                held[pl.ds((dy * Z + dz) * rows, rows), :] = jnp.where(lax.div(oz, X) == c, block_here, block_there)

    g = lax.dot_general(held[...], cot_ref[...], (((1,), (1,)), ((), ())), preferred_element_type=f32)
    place = lambda dy, dz: g[(dy * Z + dz % Z) * rows :][:rows]
    for out, places in zip(outs, units):
        turn = units is Y_FIRST and places[0][1] in ODD
        for i, (dy, dz) in enumerate(places):
            piece = jnp.where(z_odd, place(dy, dz - 2), place(dy, dz)) if turn else place(dy, dz)
            out[i * rows : (i + 1) * rows, :] = piece.astype(out.dtype)


def gradient(units, mine, other, cotangent, here, tile, start, stop):
    half, tokens = mine.shape
    ff = min(stop * tile, cotangent.shape[1]) - start * tile
    rows = 2 * half // (Z * Y)
    shapes = [(len(places) * rows, bf16 if k in (Y_ROUNDED if units is Y_FIRST else Z_ROUNDED) else f32) for k, places in enumerate(units)]
    held_in = pltpu.with_memory_space_constraint
    return pl.pallas_call(
        functools.partial(grad_kernel, units),
        grid=(stop - start,),
        in_specs=[
            pl.BlockSpec(memory_space=pltpu.SMEM),
            pl.BlockSpec(memory_space=pltpu.VMEM),
            pl.BlockSpec(memory_space=pltpu.VMEM),
            pl.BlockSpec((tile, tokens), lambda i: (start + i, 0)),
        ],
        out_specs=[pl.BlockSpec((n, tile), lambda i: (0, i)) for n, _ in shapes],
        out_shape=[(pltpu.HBM if k > 1 else pltpu.VMEM)((n, ff), t) for k, (n, t) in enumerate(shapes)],
        scratch_shapes=[pltpu.VMEM((2 * half, tokens), bf16)],
        compiler_params=pltpu.CompilerParams(vmem_limit_bytes=20 * 2**20),
        cost_estimate=pl.CostEstimate(
            flops=4 * half * tokens * ff, bytes_accessed=2 * tokens * ff + 14 * half * ff // 2, transcendentals=0
        ),
    )(here, held_in(mine, pltpu.VMEM), held_in(other, pltpu.VMEM), held_in(cotangent.T, pltpu.HBM))


def near_order(rank):
    c, x = lax.axis_index("c"), lax.axis_index("x")
    part = rank // (X * C)
    n = lax.broadcasted_iota(jnp.int32, (rank, rank), 0)
    r = lax.broadcasted_iota(jnp.int32, (rank, rank), 1)
    chunk = ((c + n // (part * X)) % C) * X + (x + (n // part) % X) % X
    return (r == chunk * part + n % part).astype(bf16)


def project(tokens, basis, beside):
    rank = basis.shape[1]
    half, part = rank // C, rank // (X * C)
    lanes = (((1,), (1,)), ((), ()))
    ordered = lax.dot_general(near_order(rank), basis, lanes, preferred_element_type=f32).astype(bf16)
    away = lax.dot_general(ordered[half:], tokens, lanes, preferred_element_type=f32)
    sent = moved(away, "c", 1)
    both = lax.dot_general(ordered[:half], tokens, lanes, preferred_element_type=f32) + sent
    total = both[:part]
    for got in [moved(both[d * part : (d + 1) * part].astype(bf16), "x", d) for d in (1, 3, 2)]:
        total = total + got.astype(f32)
    mine = total.astype(bf16)
    got = {d: moved(mine, "x", d) for d in (1, 3, 2)}
    mine, beside = lax.optimization_barrier((jnp.concatenate([mine, got[1], got[2], got[3]], 0), beside))
    return mine, moved(mine, "c", 1), beside


def scatter(ring, relay):
    four, five, k3, k6, k2, k7, k1, k0 = ring()
    up, down = moved(four, "z", 1), moved(five, "z", -1)
    two_low, two_high, one_low, one_high, three_low, three_high, low, high = relay()
    high_y, low_y = moved(two_low, "y", 1), moved(two_high, "y", -1)
    up = moved((k3 + up.astype(f32)).astype(bf16), "z", 1)
    down = moved((k6 + down.astype(f32)).astype(bf16), "z", -1)
    one = jnp.concatenate([(one_low + high_y.astype(f32)).astype(bf16), one_high], 0)
    three = jnp.concatenate([three_low, (three_high + low_y.astype(f32)).astype(bf16)], 0)
    across = [moved(one, "y", 1), moved(three, "y", -1)]
    up, down = (k2 + up.astype(f32)).astype(bf16), (k7 + down.astype(f32)).astype(bf16)
    up, down = moved(up, "z", 1), moved(down, "z", -1)
    h = low.shape[0]
    rows = h // 4
    for got in across:
        high = high + got[h:].astype(f32)
    pair = lax.ppermute(high.astype(bf16), "z", [(z, z ^ 1) for z in range(Z)])
    up = moved((k1 + up.astype(f32)).astype(bf16), "z", 1)
    low = low + pair.astype(f32)
    for got in across:
        low = low + got[:h].astype(f32)
    first, low = low[:rows], low.astype(bf16)
    for k in (2, 1, 3):
        first = first + moved(low[k * rows : (k + 1) * rows], "z", 2 * k).astype(f32)
    second = k0 + up.astype(f32) + down.astype(f32)
    second, rounded = second[:rows], second.astype(bf16)
    for k in (2, 1, 3):
        second = second + moved(rounded[k * rows : (k + 1) * rows], "y", k).astype(f32)
    return jnp.concatenate([first, second], 1)


def spread(normed, beside):
    z, y, x, c = (lax.axis_index(axis) for axis in ("z", "y", "x", "c"))
    rows, ff = normed.shape
    cut = normed.reshape(rows, Y, ff // Y).transpose(1, 0, 2)
    piece = lambda k: lax.dynamic_index_in_dim(cut, (y + k) % Y, 0, keepdims=False)
    got = {d: moved(piece(d), "y", d) for d in (1, 3, 2)}
    tall = jnp.stack([piece(0), got[1], got[2], got[3]])
    got = {d: moved(tall, "x", d) for d in (1, 3, 2)}
    wide = jnp.stack([tall, got[1], got[2], got[3]])
    odd = (z + c) % 2
    half = []
    for k in range(Z // 2):
        to = (z + 2 * k + odd) % Z
        sent = lax.dynamic_index_in_dim(wide, (x - to // 2) % X, 0, keepdims=False)
        pairs = []
        for pz in range(Z):
            for pc in range(C):
                po = (pz + pc) % 2
                for r in range(Y * X):
                    if k or po:
                        pairs.append(((pz * Y * X + r) * C + pc, (((pz + 2 * k + po) % Z) * Y * X + r) * C + (pc ^ po)))
        moved_in = lax.ppermute(sent, ("z", "y", "x", "c"), pairs)
        half.append(moved_in if k else jnp.where(odd == 0, sent, moved_in))
    half, beside = lax.optimization_barrier((jnp.stack(half), beside))
    return beside, half, moved(half, "c", 1)


def spread_order(rank):
    z, y, c = (lax.axis_index(axis) for axis in ("z", "y", "c"))
    rows = rank // (Z * Y)
    n = lax.broadcasted_iota(jnp.int32, (rank, rank), 1)
    r = lax.broadcasted_iota(jnp.int32, (rank, rank), 0)
    h, k, j = n // (rank // 2), (n // (rows * Y)) % (Z // 2), (n // rows) % Y
    owner_z = (z + 2 * Z - 2 * k - (z + c + h) % 2) % Z
    want = (owner_z * Y + (y + Y - j) % Y) * rows + n % rows
    return (r == want).astype(bf16)


def shards(tokens, basis, cotangent, exp_avg, exp_avg_sq):
    rank, ff = basis.shape[1], cotangent.shape[1]
    here = jnp.stack([lax.axis_index(axis) for axis in ("z", "y", "x", "c")]).astype(jnp.int32)
    ordered = jnp.dot(basis, spread_order(rank), preferred_element_type=f32).astype(bf16)
    mine, other, ordered = project(tokens, basis, ordered)
    lanes = 128
    tile = pl.cdiv(pl.cdiv(ff, lanes), 6) * lanes
    tiles = pl.cdiv(ff, tile)
    made = functools.partial(gradient, mine=mine, other=other, cotangent=cotangent, here=here, tile=tile)
    relay = functools.partial(made, Y_FIRST, start=0, stop=tiles // 2)
    total = scatter(functools.partial(made, Z_FIRST, start=tiles // 2, stop=tiles), relay)
    total_tokens = cotangent.shape[0] * Z * Y
    grad_low = total * (1.0 / total_tokens)
    first = 0.9 * exp_avg + 0.1 * grad_low
    second = 0.999 * exp_avg_sq + 0.001 * grad_low * grad_low
    normed = (first / bias_first / (jnp.sqrt(second / bias_second) + 1e-08)).astype(bf16)
    ordered, *parts = spread(normed, ordered)
    mine, other = (part.reshape(rank // 2, ff // Y) for part in parts)
    update = jnp.dot(ordered[:, : rank // 2], mine, preferred_element_type=f32)
    update = (update + jnp.dot(ordered[:, rank // 2 :], other, preferred_element_type=f32)).astype(bf16)
    return (update, first, second)


def solution(mesh):
    fine = Mesh(np.asarray(mesh.devices).reshape(Z, Y, X, C), ("z", "y", "x", "c"))
    dp, fsdp = ("z", "y"), ("x", "c")
    in_specs = (P(dp, fsdp), P(fsdp, None), P(dp, fsdp), P(dp, fsdp), P(dp, fsdp))
    out_specs = (P(fsdp, dp), P(dp, fsdp), P(dp, fsdp))
    return jax.shard_map(shards, mesh=fine, in_specs=in_specs, out_specs=out_specs, check_vma=False)
```

```python
import functools

import numpy as np
import jax
import jax.numpy as jnp
from jax import lax
from jax.experimental import pallas as pl
from jax.experimental.pallas import tpu as pltpu
from jax.sharding import Mesh, PartitionSpec as P

bias_first = 1.0 - 0.9**10
bias_second = 1.0 - 0.999**10
Z, Y, X, C = 8, 4, 4, 2
f32, bf16 = jnp.float32, jnp.bfloat16


def moved(value, axis, by):
    n = {"z": Z, "y": Y, "x": X, "c": C}[axis]
    return lax.ppermute(value, axis, [(i, (i + by) % n) for i in range(n)])


EVEN, ODD = (0, 2, 4, 6), (1, 3, 5, 7)
Y_FIRST = [[(dy, dz) for dz in half] for dy in (2, 1, 3, 0) for half in (EVEN, ODD)]
Z_FIRST = [[(dy, dz) for dy in range(Y)] for dz in (4, 5, 3, 6, 2, 7, 1, 0)]
Y_ROUNDED, Z_ROUNDED = (0, 1, 3, 4), (0, 1)


def grad_kernel(units, here, mine_ref, other_ref, cot_ref, *rest):
    outs, held = rest[:-1], rest[-1]
    rows = held.shape[0] // (Z * Y)
    z_odd = lax.rem(here[0], 2) == 1

    @pl.when(pl.program_id(0) == 0)
    def _():
        z, y, x, c = (here[i] for i in range(4))
        for dy in range(Y):
            for dz in range(Z):
                oz, oy = lax.rem(z + dz, Z), lax.rem(y + dy, Y)
                at = pl.multiple_of(lax.rem(x + X - lax.rem(oz, X), X) * (Y * rows) + oy * rows, rows)
                block_here, block_there = mine_ref[pl.ds(at, rows), :], other_ref[pl.ds(at, rows), :]
                held[pl.ds((dy * Z + dz) * rows, rows), :] = jnp.where(lax.div(oz, X) == c, block_here, block_there)

    g = lax.dot_general(held[...], cot_ref[...], (((1,), (1,)), ((), ())), preferred_element_type=f32)
    place = lambda dy, dz: g[(dy * Z + dz % Z) * rows :][:rows]
    for out, places in zip(outs, units):
        turn = units is Y_FIRST and places[0][1] in ODD
        for i, (dy, dz) in enumerate(places):
            piece = jnp.where(z_odd, place(dy, dz - 2), place(dy, dz)) if turn else place(dy, dz)
            out[i * rows : (i + 1) * rows, :] = piece.astype(out.dtype)


def gradient(units, mine, other, cotangent, here, tile, start, stop):
    half, tokens = mine.shape
    ff = min(stop * tile, cotangent.shape[1]) - start * tile
    rows = 2 * half // (Z * Y)
    shapes = [(len(places) * rows, bf16 if k in (Y_ROUNDED if units is Y_FIRST else Z_ROUNDED) else f32) for k, places in enumerate(units)]
    held_in = pltpu.with_memory_space_constraint
    return pl.pallas_call(
        functools.partial(grad_kernel, units),
        grid=(stop - start,),
        in_specs=[
            pl.BlockSpec(memory_space=pltpu.SMEM),
            pl.BlockSpec(memory_space=pltpu.VMEM),
            pl.BlockSpec(memory_space=pltpu.VMEM),
            pl.BlockSpec((tile, tokens), lambda i: (start + i, 0)),
        ],
        out_specs=[pl.BlockSpec((n, tile), lambda i: (0, i)) for n, _ in shapes],
        out_shape=[(pltpu.HBM if k > 1 else pltpu.VMEM)((n, ff), t) for k, (n, t) in enumerate(shapes)],
        scratch_shapes=[pltpu.VMEM((2 * half, tokens), bf16)],
        compiler_params=pltpu.CompilerParams(vmem_limit_bytes=20 * 2**20),
        cost_estimate=pl.CostEstimate(
            flops=4 * half * tokens * ff, bytes_accessed=2 * tokens * ff + 14 * half * ff // 2, transcendentals=0
        ),
    )(here, held_in(mine, pltpu.VMEM), held_in(other, pltpu.VMEM), held_in(cotangent.T, pltpu.HBM))


def near_order(rank):
    c, x = lax.axis_index("c"), lax.axis_index("x")
    part = rank // (X * C)
    n = lax.broadcasted_iota(jnp.int32, (rank, rank), 0)
    r = lax.broadcasted_iota(jnp.int32, (rank, rank), 1)
    chunk = ((c + n // (part * X)) % C) * X + (x + (n // part) % X) % X
    return (r == chunk * part + n % part).astype(bf16)


def project(tokens, basis):
    rank = basis.shape[1]
    half, part = rank // C, rank // (X * C)
    lanes = (((1,), (1,)), ((), ()))
    ordered = lax.dot_general(near_order(rank), basis, lanes, preferred_element_type=f32).astype(bf16)
    away = lax.dot_general(ordered[half:], tokens, lanes, preferred_element_type=f32)
    sent = moved(away, "c", 1)
    both = lax.dot_general(ordered[:half], tokens, lanes, preferred_element_type=f32) + sent
    total = both[:part]
    for got in [moved(both[d * part : (d + 1) * part].astype(bf16), "x", d) for d in (1, 3, 2)]:
        total = total + got.astype(f32)
    mine = total.astype(bf16)
    got = {d: moved(mine, "x", d) for d in (1, 3, 2)}
    mine = jnp.concatenate([mine, got[1], got[2], got[3]], 0)
    return mine, moved(mine, "c", 1)


def scatter(ring, relay):
    four, five, k3, k6, k2, k7, k1, k0 = ring()
    up, down = moved(four, "z", 1), moved(five, "z", -1)
    two_low, two_high, one_low, one_high, three_low, three_high, low, high = relay()
    high_y, low_y = moved(two_low, "y", 1), moved(two_high, "y", -1)
    up = moved((k3 + up.astype(f32)).astype(bf16), "z", 1)
    down = moved((k6 + down.astype(f32)).astype(bf16), "z", -1)
    one = jnp.concatenate([(one_low + high_y.astype(f32)).astype(bf16), one_high], 0)
    three = jnp.concatenate([three_low, (three_high + low_y.astype(f32)).astype(bf16)], 0)
    across = [moved(one, "y", 1), moved(three, "y", -1)]
    up, down = (k2 + up.astype(f32)).astype(bf16), (k7 + down.astype(f32)).astype(bf16)
    up, down = moved(up, "z", 1), moved(down, "z", -1)
    h = low.shape[0]
    rows = h // 4
    for got in across:
        high = high + got[h:].astype(f32)
    pair = lax.ppermute(high.astype(bf16), "z", [(z, z ^ 1) for z in range(Z)])
    up = moved((k1 + up.astype(f32)).astype(bf16), "z", 1)
    low = low + pair.astype(f32)
    for got in across:
        low = low + got[:h].astype(f32)
    first, low = low[:rows], low.astype(bf16)
    for k in (2, 1, 3):
        first = first + moved(low[k * rows : (k + 1) * rows], "z", 2 * k).astype(f32)
    second = k0 + up.astype(f32) + down.astype(f32)
    second, rounded = second[:rows], second.astype(bf16)
    for k in (2, 1, 3):
        second = second + moved(rounded[k * rows : (k + 1) * rows], "y", k).astype(f32)
    return jnp.concatenate([first, second], 1)


def spread(normed, basis):
    z, y, x, c = (lax.axis_index(axis) for axis in ("z", "y", "x", "c"))
    rows, ff = normed.shape
    cut = normed.reshape(rows, Y, ff // Y).transpose(1, 0, 2)
    piece = lambda k: lax.dynamic_index_in_dim(cut, (y + k) % Y, 0, keepdims=False)
    got = {d: moved(piece(d), "y", d) for d in (1, 3, 2)}
    tall = jnp.stack([piece(0), got[1], got[2], got[3]])
    got = {d: moved(tall, "x", d) for d in (1, 3, 2)}
    wide, basis = lax.optimization_barrier((jnp.stack([tall, got[1], got[2], got[3]]), basis))
    ordered = jnp.dot(basis, spread_order(basis.shape[1]), preferred_element_type=f32).astype(bf16)
    odd = (z + c) % 2
    half = []
    for k in range(Z // 2):
        to = (z + 2 * k + odd) % Z
        sent = lax.dynamic_index_in_dim(wide, (x - to // 2) % X, 0, keepdims=False)
        pairs = []
        for pz in range(Z):
            for pc in range(C):
                po = (pz + pc) % 2
                for r in range(Y * X):
                    if k or po:
                        pairs.append(((pz * Y * X + r) * C + pc, (((pz + 2 * k + po) % Z) * Y * X + r) * C + (pc ^ po)))
        moved_in = lax.ppermute(sent, ("z", "y", "x", "c"), pairs)
        half.append(moved_in if k else jnp.where(odd == 0, sent, moved_in))
    half, ordered = lax.optimization_barrier((jnp.stack(half), ordered))
    return ordered, half, moved(half, "c", 1)


def spread_order(rank):
    z, y, c = (lax.axis_index(axis) for axis in ("z", "y", "c"))
    rows = rank // (Z * Y)
    n = lax.broadcasted_iota(jnp.int32, (rank, rank), 1)
    r = lax.broadcasted_iota(jnp.int32, (rank, rank), 0)
    h, k, j = n // (rank // 2), (n // (rows * Y)) % (Z // 2), (n // rows) % Y
    owner_z = (z + 2 * Z - 2 * k - (z + c + h) % 2) % Z
    want = (owner_z * Y + (y + Y - j) % Y) * rows + n % rows
    return (r == want).astype(bf16)


def shards(tokens, basis, cotangent, exp_avg, exp_avg_sq):
    rank, ff = basis.shape[1], cotangent.shape[1]
    here = jnp.stack([lax.axis_index(axis) for axis in ("z", "y", "x", "c")]).astype(jnp.int32)
    mine, other = project(tokens, basis)
    lanes = 128
    tile = pl.cdiv(pl.cdiv(ff, lanes), 6) * lanes
    tiles = pl.cdiv(ff, tile)
    made = functools.partial(gradient, mine=mine, other=other, cotangent=cotangent, here=here, tile=tile)
    relay = functools.partial(made, Y_FIRST, start=0, stop=tiles // 2)
    total = scatter(functools.partial(made, Z_FIRST, start=tiles // 2, stop=tiles), relay)
    total_tokens = cotangent.shape[0] * Z * Y
    grad_low = total * (1.0 / total_tokens)
    first = 0.9 * exp_avg + 0.1 * grad_low
    second = 0.999 * exp_avg_sq + 0.001 * grad_low * grad_low
    normed = (first / bias_first / (jnp.sqrt(second / bias_second) + 1e-08)).astype(bf16)
    ordered, *parts = spread(normed, basis)
    mine, other = (part.reshape(rank // 2, ff // Y) for part in parts)
    update = jnp.dot(ordered[:, : rank // 2], mine, preferred_element_type=f32)
    update = (update + jnp.dot(ordered[:, rank // 2 :], other, preferred_element_type=f32)).astype(bf16)
    return (update, first, second)


def solution(mesh):
    fine = Mesh(np.asarray(mesh.devices).reshape(Z, Y, X, C), ("z", "y", "x", "c"))
    dp, fsdp = ("z", "y"), ("x", "c")
    in_specs = (P(dp, fsdp), P(fsdp, None), P(dp, fsdp), P(dp, fsdp), P(dp, fsdp))
    out_specs = (P(fsdp, dp), P(dp, fsdp), P(dp, fsdp))
    return jax.shard_map(shards, mesh=fine, in_specs=in_specs, out_specs=out_specs, check_vma=False)
```
